256 devices in a mesh: grp: 32 (over y_lo, z, core), tp: 8 (over y_hi, x).
Axes of the slice: x: 4, y: 4 (y_hi: 2, y_lo: 2; y = y_hi * 2 + y_lo), z: 8, core: 2. Of those that a mesh axis runs over, the one named last changes fastest.
Arguments:
- prompt_queries: bfloat16 [2, 36864, 8192], P(None, 'grp', 'tp'), may hold values from -100 to 100
- prompt_kv: bfloat16 [2, 36864, 2048], P(None, 'grp', 'tp'), may hold values from -6 to 6
- page_table: int32 [96, 3], P('grp'), may hold values from 0 to 8, as said below
- prompt_lengths: int32 [96], P('grp'), may hold values from 1 to 384
- targets: int32 [96, 1], P('grp'), may hold values from 0 to 2; in each aligned block of 3 rows (0 to 2, 3 to 5, ...) at most 2 rows name the same one
- step_queries: bfloat16 [96, 2, 16, 1024], P('grp', None, 'tp'), may hold values from -100 to 100
- step_kv: bfloat16 [96, 2, 16, 256], P('grp', None, 'tp'), may hold values from -6 to 6
Outputs:
- prompt_out: bfloat16 [2, 36864, 8192], P(None, 'grp', 'tp')
- step_out: bfloat16 [96, 2, 16, 1024], P('grp', None, 'tp')
- cache_pool: bfloat16 [96, 2, 384, 4096], P('grp', None, None, 'tp')
The draws below stay inside these ranges and needn't reach their ends.
Inputs may be any that keep to these rules, and one draw needn't show every extreme that they name: `page_table`: the 3 rows of one group together name each of its pool pages exactly once. `targets`: among the rows of one group no value appears more than 2 times.
All inputs are finite; a program needn't handle non-finite values.
Results may differ from the reference program's by a relative error of at most 0.011.
Values may be sent and summed in bfloat16 or wider, within the bound.
No kernel may reach another device: no remote copies, remote signals or barrier semaphores. Data moves between devices by JAX's collectives and lax.ppermute only.
A program may use at most 128 MiB of HBM per device.

```python
import math
import jax
import jax.numpy as jnp
import numpy as np
from jax import lax

Q_HEADS = 64
KV_HEADS = 8
HD = 128
PAGE = 128
PAGES_P = 3
PROMPTS_DEV = 3
LAYERS = 2
NEAR = 3
CAP = 2
PROMPT = 384
PROMPTS = 96
POOL_TOKENS = 36864
SLOTS = 96
N_GRP = 32
N_TP = 8


def query_values(key, shape):
    values = jnp.clip(jax.random.normal(key, shape, jnp.float32), -6.0, 6.0)
    return values.astype(jnp.bfloat16)


def draw_prompt_queries(key, part):
    key = jax.random.fold_in(key, 11)
    return query_values(key, (LAYERS, POOL_TOKENS, Q_HEADS * HD))


def draw_step_queries(key, part):
    key = jax.random.fold_in(key, 12)
    return query_values(key, (SLOTS, LAYERS, CAP * KV_HEADS, Q_HEADS // KV_HEADS * HD))


def draw_page_table(key, part):
    key = jax.random.fold_in(key, 13)
    group_keys = jax.random.split(key, N_GRP)
    orders = jax.vmap(lambda single: jax.random.permutation(single, PROMPTS_DEV * PAGES_P))(group_keys)
    return orders.reshape(PROMPTS, PAGES_P).astype(jnp.int32)


def draw_prompt_lengths(key, part):
    key = jax.random.fold_in(key, 14)
    first_key, second_key = jax.random.split(key)
    lengths = jax.random.randint(first_key, (PROMPTS,), 1, PROMPT + 1)
    longest = jax.random.randint(second_key, (), 0, PROMPTS)
    return jnp.where(jnp.arange(PROMPTS) == longest, PROMPT, lengths).astype(jnp.int32)


def steps_of(stream_key, shape, cuts, smallest, high):
    gain = 1.0
    for position, shards_of in cuts:
        heights = jax.random.uniform(jax.random.fold_in(jax.random.fold_in(stream_key, 6), position), (shards_of,), jnp.float32, smallest / len(cuts), high / len(cuts))
        gain = gain * jnp.repeat(jnp.exp(heights), shape[position] // shards_of).reshape((-1,) + (1,) * (len(shape) - 1 - position))
    return gain


def shared_out(key, own, number, rows, number_of, top, reach, skew):
    sequence = jax.random.permutation(key, number_of)
    packed, common = shares(number_of, rows * top, reach, skew, True), shares(number_of, rows * top, reach, skew, False)
    places = jnp.arange(number_of)

    def named(sizes, rotation):
        used = int((sizes > 0).sum())
        fixed = max(1, used // 4)
        shifted = fixed + (places - fixed + rotation * (used - fixed)) % max(1, number_of - fixed)
        return jnp.zeros((number_of,), jnp.int32).at[sequence[jnp.where(places < fixed, places, shifted)]].set(jnp.asarray(sizes, jnp.int32))

    sizes = jnp.where(number % 4 == 0, named(packed, number // 4), named(common, number - number // 4 - 1))
    mixed = jax.random.permutation(jax.random.fold_in(own, 3), number_of)
    donor, sink = mixed[0:number_of // 2 * 2:2], mixed[1:number_of // 2 * 2:2]
    slack = jnp.minimum(sizes[donor] - 1, reach - sizes[sink]) // 2
    slack = jnp.where((donor == sequence[0]) | (sink == sequence[0]) | (sizes[sink] == 0), 0, jnp.maximum(slack, 0))
    shifted = jax.random.randint(jax.random.fold_in(own, 4), (number_of // 2,), 0, 1 << 20) % (slack + 1)
    sizes = sizes.at[donor].add(-shifted).at[sink].add(shifted)
    labels = jnp.searchsorted(jnp.cumsum(sizes), jnp.arange(rows * top), side="right").astype(jnp.int32)
    table = labels.reshape(top, rows).T
    table = table[jax.random.permutation(jax.random.fold_in(own, 1), rows)]
    rotation = jax.random.randint(jax.random.fold_in(own, 2), (rows, 1), 0, top)
    return jnp.take_along_axis(table, (jnp.arange(top)[None, :] + rotation) % top, axis=1)


def shares(count, total, reach, lean, full):
    weights = [(1 << 20) // math.isqrt(grade ** lean) + 1 for grade in range(1, count + 1)]
    largest = reach if full else min(reach, max(-(-total // count), total * weights[0] // sum(weights)))
    least = 1 if total - largest >= count - 1 else 0
    given, spare = [largest] + [least] * (count - 1), total - largest - least * (count - 1)
    while spare > 0:
        free = [i for i in range(1, count) if given[i] < largest] or [i for i in range(1, count) if given[i] < reach]
        pool, remaining = sum([weights[i] for i in free]), spare
        for i in free:
            more = min(reach - given[i], max(1, remaining * weights[i] // pool), spare)
            given[i] = given[i] + more
            spare = spare - more
    return np.array(given)


def normal_values(stream_key, dims, deviation, most, cuts=(), held_as=jnp.bfloat16):
    entries = deviation * jax.random.normal(stream_key, dims, jnp.float32)
    if cuts:
        entries = entries * steps_of(stream_key, dims, cuts, -0.22, 0.18)
    return jnp.clip(entries, -most, most).astype(held_as)


def setup_inputs(seed: int = 0) -> dict:
    arg_keys = jax.random.split(jax.random.key(seed), 8)
    prompt_queries = draw_prompt_queries(jax.random.fold_in(arg_keys[7], 71), 0)
    prompt_kv = normal_values(arg_keys[1], (LAYERS, POOL_TOKENS, KV_HEADS * 2 * HD), 1.0, 6.0, ((1, 32), (2, 8)))
    page_table = draw_page_table(jax.random.fold_in(arg_keys[7], 71), 0)
    prompt_lengths = draw_prompt_lengths(jax.random.fold_in(arg_keys[7], 71), 0)
    targets_keys = jax.random.split(jax.random.fold_in(arg_keys[4], 1), PROMPTS // PROMPTS_DEV)
    targets_turns = jax.random.permutation(jax.random.fold_in(arg_keys[4], 3), PROMPTS // PROMPTS_DEV)
    targets = jax.vmap(lambda own, number: shared_out(jax.random.fold_in(arg_keys[4], 2), own, number, PROMPTS_DEV, NEAR, 1, CAP, 1))(targets_keys, targets_turns).reshape((PROMPTS, 1))
    step_queries = draw_step_queries(jax.random.fold_in(arg_keys[7], 71), 0)
    step_kv = normal_values(arg_keys[6], (SLOTS, LAYERS, CAP * KV_HEADS, 2 * HD), 1.0, 6.0, ((0, 32), (2, 8)))
    return {"prompt_queries": prompt_queries, "prompt_kv": prompt_kv, "page_table": page_table, "prompt_lengths": prompt_lengths, "targets": targets, "step_queries": step_queries, "step_kv": step_kv}


masked_score = -1e+30

def rotate(inputs, positions):
    halfway = inputs.shape[-1] // 2
    inverse = jnp.exp(jnp.arange(halfway, dtype=jnp.float32) * (-2.0 * math.log(500000.0) / inputs.shape[-1]))
    angles = positions[..., None] * inverse
    cosine = jnp.cos(angles)
    sine_part = jnp.sin(angles)
    lower_half = inputs[..., :halfway]
    upper_half = inputs[..., halfway:]
    return jnp.concatenate([lower_half * cosine - upper_half * sine_part, upper_half * cosine + lower_half * sine_part], axis=-1)

def slot_ranks(rows, earlier):
    return lax.optimization_barrier(jnp.sum((rows[..., None, :] == rows[..., :, None]) & earlier, axis=-1)).astype(jnp.int32)

def prompt_layer(queries, keys_values, page_rows, lengths):
    page_count, pages_each = page_rows.shape
    extent = pages_each * PAGE
    head_count = keys_values.shape[-1] // (2 * HD)
    group_size = Q_HEADS // KV_HEADS
    q_tok = queries.reshape(-1, PAGE, queries.shape[-1])[page_rows].reshape(page_count, extent, head_count, group_size, HD)
    kv_tok = keys_values.reshape(-1, PAGE, head_count, 2, HD)[page_rows].reshape(page_count, extent, head_count, 2, HD)
    positions = jnp.arange(extent).astype(jnp.float32)
    q_rot = rotate(q_tok.astype(jnp.float32), positions[None, :, None, None]).astype(jnp.bfloat16)
    k_rot = rotate(kv_tok[..., 0, :].astype(jnp.float32), positions[None, :, None]).astype(jnp.bfloat16)
    values = kv_tok[..., 1, :]
    scores = jnp.einsum('pqhgd,pkhd->phgqk', q_rot.astype(jnp.float32), k_rot.astype(jnp.float32)) * (1.0 / math.sqrt(HD))
    token_index = jnp.arange(extent)
    in_prompt = token_index[None, :] < lengths[:, None]
    allowed = (token_index[:, None] >= token_index[None, :])[None] & in_prompt[:, None, :]
    scores = jnp.where(allowed[:, None, None], scores, masked_score)
    maximum = lax.optimization_barrier(jnp.max(scores, axis=-1, keepdims=True))
    exponent = jnp.exp(scores - maximum)
    weights = (exponent / lax.optimization_barrier(jnp.sum(exponent, axis=-1, keepdims=True))).astype(jnp.bfloat16)
    attended = jnp.einsum('phgqk,pkhd->pqhgd', weights.astype(jnp.float32), values.astype(jnp.float32))
    attended = jnp.where(in_prompt[:, :, None, None, None], attended, 0.0).astype(jnp.bfloat16)
    outgoing = jnp.where(in_prompt[:, :, None, None, None], jnp.stack([k_rot, values], axis=3), jnp.zeros((), jnp.bfloat16))
    return (attended.reshape(page_count * extent, -1), outgoing)

def step_attend(queries, fresh_kv, cached, lengths):
    extent = cached.shape[1]
    scaling = 1.0 / math.sqrt(HD)
    positions = lengths.astype(jnp.float32)
    q_rot = rotate(queries.astype(jnp.float32), positions[:, None, None]).astype(jnp.bfloat16)
    k_new = rotate(fresh_kv[..., 0, :].astype(jnp.float32), positions[:, None]).astype(jnp.bfloat16)
    scores = jnp.einsum('khgd,kthd->khgt', q_rot.astype(jnp.float32), cached[..., 0, :].astype(jnp.float32)) * scaling
    in_cache = jnp.arange(extent)[None, :] < lengths[:, None]
    scores = jnp.where(in_cache[:, None, None, :], scores, masked_score)
    own_score = lax.optimization_barrier(jnp.sum(q_rot.astype(jnp.float32) * k_new[:, :, None, :].astype(jnp.float32), axis=-1)) * scaling
    maximum = jnp.maximum(lax.optimization_barrier(jnp.max(scores, axis=-1)), own_score)
    exponent = jnp.exp(scores - maximum[..., None])
    own_exp = jnp.exp(own_score - maximum)
    denominator = lax.optimization_barrier(jnp.sum(exponent, axis=-1)) + own_exp
    weights = (exponent / denominator[..., None]).astype(jnp.bfloat16)
    own_weight = (own_exp / denominator).astype(jnp.bfloat16)
    result = jnp.einsum('khgt,kthd->khgd', weights.astype(jnp.float32), cached[..., 1, :].astype(jnp.float32))
    result = result + own_weight[..., None].astype(jnp.float32) * fresh_kv[:, :, None, 1, :].astype(jnp.float32)
    return result.astype(jnp.bfloat16)

def reference(prompt_queries, prompt_kv, page_table, prompt_lengths, targets, step_queries, step_kv):
    groups = N_GRP
    group_size = Q_HEADS // KV_HEADS
    pool_len = PROMPTS_DEV * PROMPT
    q_all = prompt_queries.reshape(LAYERS, groups, pool_len, Q_HEADS * HD).transpose(1, 0, 2, 3)
    kv_all = prompt_kv.reshape(LAYERS, groups, pool_len, KV_HEADS * 2 * HD).transpose(1, 0, 2, 3)
    tables = page_table.reshape(groups, PROMPTS_DEV, PAGES_P)
    length_rows = prompt_lengths.reshape(groups, PROMPTS_DEV)

    def one_group(items):
        q_group, kv_group, table_group, length_group = items
        results = [prompt_layer(q_group[l], kv_group[l], table_group, length_group) for l in range(LAYERS)]
        return (jnp.stack([item[0] for item in results]), jnp.stack([item[1] for item in results]))
    attended, outgoing = lax.map(one_group, (q_all, kv_all, tables, length_rows))
    prompt_out = attended.transpose(1, 0, 2, 3).reshape(LAYERS, groups * pool_len, Q_HEADS * HD)
    route_rows = targets[:, 0].reshape(groups, PROMPTS_DEV)
    earlier = jnp.arange(PROMPTS_DEV)[None, :] < jnp.arange(PROMPTS_DEV)[:, None]
    rank_rows = slot_ranks(route_rows, earlier)
    pair_size = 2 * KV_HEADS // N_TP
    halves = N_TP // 2
    query_all = step_queries.reshape(groups, NEAR, LAYERS, halves, CAP, pair_size, group_size, HD)
    fresh_all = step_kv.reshape(groups, NEAR, LAYERS, halves, CAP, pair_size, 2, HD)

    def one_decode(items):
        decode_group, query_group, fresh_group = items
        caches = []
        lengths = []
        for k in range(NEAR):
            source = (decode_group - 1 - k) % groups
            sent_rows = lax.dynamic_index_in_dim(outgoing, source, 0, False)
            route_row = lax.dynamic_index_in_dim(route_rows, source, 0, False)
            rank_row = lax.dynamic_index_in_dim(rank_rows, source, 0, False)
            length_row = lax.dynamic_index_in_dim(length_rows, source, 0, False)
            chosen = (route_row == k)[None, :] & (rank_row[None, :] == jnp.arange(CAP)[:, None])
            caches.append(jnp.einsum('cp,lpthvd->clthvd', chosen.astype(jnp.float32), sent_rows.astype(jnp.float32)).astype(jnp.bfloat16))
            lengths.append(lax.optimization_barrier(jnp.sum(jnp.where(chosen, length_row[None, :], 0), axis=-1)).astype(jnp.int32))
        cached = jnp.stack(caches)
        held = jnp.stack(lengths)
        queries = query_group.transpose(0, 3, 1, 2, 4, 5, 6).reshape(NEAR, CAP, LAYERS, KV_HEADS, group_size, HD)
        fresh_kv = fresh_group.transpose(0, 3, 1, 2, 4, 5, 6).reshape(NEAR, CAP, LAYERS, KV_HEADS, 2, HD)
        step_rows = []
        for l in range(LAYERS):
            result = step_attend(queries[:, :, l].reshape(NEAR * CAP, KV_HEADS, group_size, HD), fresh_kv[:, :, l].reshape(NEAR * CAP, KV_HEADS, 2, HD), cached[:, :, l].reshape(NEAR * CAP, PROMPT, KV_HEADS, 2, HD), held.reshape(-1))
            step_rows.append(result.reshape(NEAR, CAP, halves, pair_size, group_size, HD))
        step_group = jnp.stack(step_rows, axis=1).transpose(0, 1, 3, 2, 4, 5, 6).reshape(NEAR, LAYERS, CAP * KV_HEADS, group_size * HD)
        pool_group = cached.reshape(NEAR, CAP, LAYERS, PROMPT, halves, pair_size, 2, HD).transpose(0, 2, 3, 4, 1, 5, 6, 7).reshape(NEAR, LAYERS, PROMPT, CAP * KV_HEADS * 2 * HD)
        return (step_group, pool_group)
    step_group, pool_group = lax.map(one_decode, (jnp.arange(groups).astype(jnp.int32), query_all, fresh_all))
    step_out = step_group.reshape(groups * NEAR, LAYERS, CAP * KV_HEADS, group_size * HD)
    cache_pool = pool_group.reshape(groups * NEAR, LAYERS, PROMPT, CAP * KV_HEADS * 2 * HD)
    return (prompt_out, step_out, cache_pool)
```

```python
import functools
import math

import jax
import jax.numpy as jnp
import numpy as np
from jax import lax
from jax.experimental import pallas as pl
from jax.experimental.pallas import tpu as pltpu
from jax.sharding import PartitionSpec as P

Q_HEADS = 64
KV_HEADS = 8
GROUP = Q_HEADS // KV_HEADS
HD = 128
PAGE = 128
PAGES_P = 3
PROMPTS_DEV = 3
PROMPT = PAGE * PAGES_P
POOL = PROMPTS_DEV * PROMPT
LAYERS = 2
NEAR = 3
CAP = 2
N_GRP = 32
N_TP = 8

LENGTHS_AT = PROMPTS_DEV * PAGES_P
TARGETS_AT = LENGTHS_AT + PROMPTS_DEV
PLACE_AT = TARGETS_AT + PROMPTS_DEV

masked_score = -1e30
EXP2_SCALE = math.log2(math.e) / math.sqrt(HD)
VMEM_LIMIT = 48 * 1024 * 1024


def rotary_tables():
    halfway = HD // 2
    inverse = np.exp(
        np.arange(halfway, dtype=np.float32) * np.float32(-2.0 * math.log(500000.0) / HD)
    ).astype(np.float32)
    angles = (np.arange(PROMPT + 8, dtype=np.float32)[:, None] * inverse).astype(np.float64)
    cosine = np.cos(angles).astype(np.float32)
    sine = np.sin(angles).astype(np.float32)
    return np.concatenate([cosine, cosine], axis=1), np.concatenate([-sine, sine], axis=1)


def rotated(values, cosine, sine):
    return values * cosine + pltpu.roll(values, HD // 2, 1) * sine


def nt_dot(left, right):
    return lax.dot_general(left, right, (((1,), (1,)), ((), ())), preferred_element_type=jnp.float32)


def picked(plan, target, rank):
    index = jnp.int32(0)
    found = jnp.int32(0)
    before = jnp.int32(0)
    for r in range(PROMPTS_DEV):
        same = (plan[TARGETS_AT + r] == target).astype(jnp.int32)
        hit = same * (before == rank).astype(jnp.int32)
        index = index + hit * r
        found = found + hit
        before = before + same
    return found * plan[LENGTHS_AT + index], [plan[index * PAGES_P + j] for j in range(PAGES_P)]


def attend_kernel(plan, q_ref, k0_ref, k1_ref, k2_ref, cos_ref, sin_ref, *rest, first):
    out_ref, krot, vext = rest[-3:]
    prompt = first + pl.program_id(0)
    page = pl.program_id(1)
    length = plan[LENGTHS_AT + lax.rem(prompt, PROMPTS_DEV)]

    @pl.when(page == 0)
    def _():
        for j, ref in enumerate((k0_ref, k1_ref, k2_ref)):
            rows = slice(j * PAGE, (j + 1) * PAGE)
            keys = ref[0, :, :HD].astype(jnp.float32)
            krot[rows, :] = rotated(keys, cos_ref[rows, :], sin_ref[rows, :]).astype(jnp.bfloat16)
            vext[rows, :HD] = ref[0, :, HD:]
        vext[:, HD:] = jnp.ones((PROMPT, HD), jnp.bfloat16)

    start = page * PAGE

    @pl.when(start >= length)
    def _():
        out_ref[...] = jnp.zeros_like(out_ref)

    def block(count):
        keys = count * PAGE
        rows = slice(keys - PAGE, keys)
        cosine = cos_ref[rows, :]
        sine = sin_ref[rows, :]
        row = lax.broadcasted_iota(jnp.int32, (PAGE, PAGE), 0)
        causal = row >= lax.broadcasted_iota(jnp.int32, (PAGE, PAGE), 1)
        in_prompt = row + (keys - PAGE) < length
        for h in range(GROUP):
            lanes = slice(h * HD, (h + 1) * HD)
            query = rotated(q_ref[0, :, lanes].astype(jnp.float32), cosine, sine)
            scores = nt_dot(query.astype(jnp.bfloat16), krot[:keys, :])
            own = jnp.where(causal, scores[:, keys - PAGE :], masked_score)
            if count > 1:
                scores = jnp.concatenate([scores[:, : keys - PAGE], own], axis=1)
            else:
                scores = own
            maximum = jnp.max(scores, axis=1, keepdims=True)
            weights = jnp.exp2((scores - maximum) * EXP2_SCALE).astype(jnp.bfloat16)
            total = jnp.dot(weights, vext[:keys, :], preferred_element_type=jnp.float32)
            result = jnp.where(in_prompt, total[:, :HD] / total[:, HD:], 0.0)
            out_ref[0, :, lanes] = result.astype(jnp.bfloat16)

    for count in range(1, PAGES_P + 1):
        pl.when((page == count - 1) & (start < length))(functools.partial(block, count))


def attend(plan, queries, keys_values, cosine, sine, earlier, first, count):
    def layer(i):
        return (first + i) // PROMPTS_DEV

    def q_map(i, page, plan):
        return (layer(i), plan[lax.rem(first + i, PROMPTS_DEV) * PAGES_P + page], 0)

    def kv_map(j):
        return lambda i, page, plan: (layer(i), plan[lax.rem(first + i, PROMPTS_DEV) * PAGES_P + j], 0)

    def out_map(i, page, plan):
        return (layer(i), lax.rem(first + i, PROMPTS_DEV) * PAGES_P + page, 0)

    table = pl.BlockSpec((PROMPT, HD), lambda i, page, plan: (0, 0))
    in_specs = [pl.BlockSpec((1, PAGE, GROUP * HD), q_map)]
    in_specs += [pl.BlockSpec((1, PAGE, 2 * HD), kv_map(j)) for j in range(PAGES_P)]
    in_specs += [table, table]
    operands = [plan, queries, keys_values, keys_values, keys_values, cosine, sine]
    aliases = {}
    if earlier is not None:
        in_specs.append(pl.BlockSpec(memory_space=pl.ANY))
        aliases = {len(operands): 0}
        operands.append(earlier)
    return pl.pallas_call(
        functools.partial(attend_kernel, first=first),
        grid_spec=pltpu.PrefetchScalarGridSpec(
            num_scalar_prefetch=1,
            grid=(count, PAGES_P),
            in_specs=in_specs,
            out_specs=pl.BlockSpec((1, PAGE, GROUP * HD), out_map),
            scratch_shapes=[
                pltpu.VMEM((PROMPT, HD), jnp.bfloat16),
                pltpu.VMEM((PROMPT, 2 * HD), jnp.bfloat16),
            ],
        ),
        out_shape=jax.ShapeDtypeStruct(queries.shape, jnp.bfloat16),
        input_output_aliases=aliases,
        cost_estimate=pl.CostEstimate(
            flops=count * GROUP * 6 * PAGE * PAGE * HD * 4 * 4,
            bytes_accessed=count * PROMPT * GROUP * HD * 4,
            transcendentals=count * GROUP * 6 * PAGE * PAGE,
        ),
        compiler_params=pltpu.CompilerParams(vmem_limit_bytes=VMEM_LIMIT),
        name="attend",
    )(*operands)


def write_unit(out_ref, source, length, pages, cos_ref, sin_ref):
    for j in range(PAGES_P):
        rows = slice(j * PAGE, (j + 1) * PAGE)
        page = source[pl.ds(pl.multiple_of(pages[j] * PAGE, PAGE), PAGE), :]
        inside = lax.broadcasted_iota(jnp.int32, (PAGE, HD), 0) + j * PAGE < length
        keys = rotated(page[:, :HD].astype(jnp.float32), cos_ref[rows, :], sin_ref[rows, :])
        values = page[:, HD:].astype(jnp.float32)
        out_ref[rows, :HD] = jnp.where(inside, keys, 0.0).astype(jnp.bfloat16)
        out_ref[rows, HD:] = jnp.where(inside, values, 0.0).astype(jnp.bfloat16)


def pack_kernel(plan, plan2, own_ref, got_ref, cos_ref, sin_ref, *outs):
    core = plan[PLACE_AT] // 2
    column = lax.rem(plan[PLACE_AT], 2)
    local, near_same, near_other, mid_other, far_same, far_other = outs
    write = functools.partial(write_unit, cos_ref=cos_ref, sin_ref=sin_ref)

    @pl.when(core == 0)
    def _():
        write(near_same, own_ref.at[0], *picked(plan, 0, column))
        write(near_other, own_ref.at[0], *picked(plan, 0, 1 - column))

    @pl.when(core == 1)
    def _():
        write(near_same, got_ref, *picked(plan2, 0, column))
        write(near_other, got_ref, *picked(plan2, 0, 1 - column))

    write(local, got_ref, *picked(plan2, 1, column))
    write(mid_other, got_ref, *picked(plan2, 1, 1 - column))
    write(far_same, got_ref, *picked(plan2, 2, column))
    write(far_other, got_ref, *picked(plan2, 2, 1 - column))


def pack(plan, plan2, keys_values, got, cosine, sine, layer):
    table = pl.BlockSpec((PROMPT, HD), lambda i, *_: (0, 0))
    unit = jax.ShapeDtypeStruct((PROMPT, 2 * HD), jnp.bfloat16)
    return pl.pallas_call(
        pack_kernel,
        grid_spec=pltpu.PrefetchScalarGridSpec(
            num_scalar_prefetch=2,
            grid=(1,),
            in_specs=[
                pl.BlockSpec((1, POOL, 2 * HD), lambda i, *_: (layer, 0, 0)),
                pl.BlockSpec((POOL, 2 * HD), lambda i, *_: (0, 0)),
                table,
                table,
            ],
            out_specs=[pl.BlockSpec((PROMPT, 2 * HD), lambda i, *_: (0, 0))] * 6,
        ),
        out_shape=[unit] * 6,
        cost_estimate=pl.CostEstimate(flops=10**6, bytes_accessed=3 * 10**6, transcendentals=0),
        compiler_params=pltpu.CompilerParams(vmem_limit_bytes=VMEM_LIMIT),
        name="pack",
    )(plan, plan2, keys_values, got, cosine, sine)


def settle_kernel(plan, plan1, plan2, plan3, *refs):
    units, (q_ref, kv_ref, cos_ref, sin_ref) = refs[:6], refs[6:10]
    pool_ref, step_ref = refs[-2:]
    column = lax.rem(plan[PLACE_AT], 2)

    for k, arrived in enumerate((plan1, plan2, plan3)):
        held, _ = picked(arrived, k, column)
        cosine = cos_ref[pl.ds(held, 1), :]
        sine = sin_ref[pl.ds(held, 1), :]
        inside = lax.broadcasted_iota(jnp.int32, (GROUP, PROMPT), 1) < held
        for part in range(2):
            unit = units[2 * k + part]
            head = column if part == 0 else 1 - column
            pool_ref[k, 0, :, pl.ds(pl.multiple_of(head * 2 * HD, 2 * HD), 2 * HD)] = unit[...]
            rows = q_ref[k, 0, :, :].astype(jnp.float32)
            row = jnp.where(head == 0, rows[:1], rows[1:])
            query = jnp.concatenate([row[:, g * HD : (g + 1) * HD] for g in range(GROUP)], axis=0)
            query = rotated(query, cosine, sine).astype(jnp.bfloat16)
            rows = kv_ref[k, 0, :, :].astype(jnp.float32)
            fresh = jnp.where(head == 0, rows[:1], rows[1:])
            key = jnp.broadcast_to(fresh[:, :HD], (8, HD))
            key = rotated(key, cosine, sine).astype(jnp.bfloat16).astype(jnp.float32)
            scores = jnp.where(inside, nt_dot(query, unit[:, :HD]), masked_score)
            own = jnp.sum(query.astype(jnp.float32) * key, axis=1, keepdims=True)
            maximum = jnp.maximum(jnp.max(scores, axis=1, keepdims=True), own)
            exponent = jnp.exp2((scores - maximum) * EXP2_SCALE)
            own = jnp.exp2((own - maximum) * EXP2_SCALE)
            total = jnp.sum(exponent, axis=1, keepdims=True) + own
            weights = (exponent / total).astype(jnp.bfloat16)
            own = (own / total).astype(jnp.bfloat16).astype(jnp.float32)
            result = jnp.dot(weights, unit[:, HD:], preferred_element_type=jnp.float32)
            result = result + own * fresh[:, HD:]
            step_ref[k, pl.ds(head, 1), :] = jnp.concatenate(
                [result[g : g + 1, :] for g in range(GROUP)], axis=1
            )


def settle(plans, units, step_queries, step_kv, cosine, sine, pool, layer):
    whole = pl.BlockSpec((PROMPT + 8, HD), lambda i, *_: (0, 0))
    in_specs = [pl.BlockSpec((PROMPT, 2 * HD), lambda i, *_: (0, 0))] * 6
    in_specs += [
        pl.BlockSpec((NEAR, 1, 2, GROUP * HD), lambda i, *_: (0, layer, 0, 0)),
        pl.BlockSpec((NEAR, 1, 2, 2 * HD), lambda i, *_: (0, layer, 0, 0)),
        whole,
        whole,
    ]
    operands = [*plans, *units, step_queries, step_kv, cosine, sine]
    aliases = {}
    if pool is not None:
        in_specs.append(pl.BlockSpec(memory_space=pl.ANY))
        aliases = {len(operands): 0}
        operands.append(pool)
    return pl.pallas_call(
        settle_kernel,
        grid_spec=pltpu.PrefetchScalarGridSpec(
            num_scalar_prefetch=len(plans),
            grid=(1,),
            in_specs=in_specs,
            out_specs=[
                pl.BlockSpec((NEAR, 1, PROMPT, 4 * HD), lambda i, *_: (0, layer, 0, 0)),
                pl.BlockSpec((NEAR, 2, GROUP * HD), lambda i, *_: (0, 0, 0)),
            ],
        ),
        out_shape=[
            jax.ShapeDtypeStruct((NEAR, LAYERS, PROMPT, 4 * HD), jnp.bfloat16),
            jax.ShapeDtypeStruct((NEAR, 2, GROUP * HD), jnp.float32),
        ],
        input_output_aliases=aliases,
        cost_estimate=pl.CostEstimate(flops=10**7, bytes_accessed=3 * 10**6, transcendentals=0),
        compiler_params=pltpu.CompilerParams(vmem_limit_bytes=VMEM_LIMIT),
        name="settle",
    )(*operands)


def moved(value, by, flip, only=None):
    pairs = []
    for g in range(N_GRP):
        target = g ^ 1 if by is None else (g + by) % N_GRP
        for t in range(N_TP):
            pairs.append((g * N_TP + t, target * N_TP + (t ^ flip)))
    return lax.ppermute(value, ("grp", "tp"), pairs)


def on_device(
    prompt_queries, prompt_kv, page_table, prompt_lengths, targets, step_queries, step_kv
):
    cosine, sine = (jnp.asarray(table) for table in rotary_tables())
    place = lax.axis_index("grp") % 2 * 2 + lax.axis_index("tp") % 2
    plan = jnp.concatenate(
        [page_table.reshape(-1), prompt_lengths, targets.reshape(-1), place.reshape(1).astype(jnp.int32)]
    )
    got = [moved(prompt_kv[l], 2, 0) for l in range(LAYERS)]
    plans = [plan] + [moved(plan, k + 1, 0) for k in range(NEAR)]

    out = attend(plan, prompt_queries, prompt_kv, cosine, sine, None, 0, 3)
    units = []
    for l in range(LAYERS):
        local, near_same, near_other, mid_other, far_same, far_other = pack(
            plan, plans[2], prompt_kv, got[l], cosine, sine, l
        )
        units.append(
            [
                moved(near_same, None, 0),
                moved(near_other, None, 1),
                local,
                moved(mid_other, 0, 1),
                moved(far_same, 1, 0),
                moved(far_other, 1, 1),
            ]
        )
    out = attend(plan, prompt_queries, prompt_kv, cosine, sine, out, 3, 3)
    pool = None
    steps = []
    for l in range(LAYERS):
        pool, step = settle(plans, units[l], step_queries, step_kv, cosine, sine, pool, l)
        steps.append(step)
    return out, jnp.stack(steps, axis=1).astype(jnp.bfloat16), pool


def solution(mesh):
    return jax.shard_map(
        on_device,
        mesh=mesh,
        in_specs=(
            P(None, "grp", "tp"),
            P(None, "grp", "tp"),
            P("grp", None),
            P("grp"),
            P("grp", None),
            P("grp", None, "tp", None),
            P("grp", None, "tp", None),
        ),
        out_specs=(P(None, "grp", "tp"), P("grp", None, "tp", None), P("grp", None, None, "tp")),
        check_vma=False,
    )
```

```python
import functools
import math

import jax
import jax.numpy as jnp
import numpy as np
from jax import lax
from jax.experimental import pallas as pl
from jax.experimental.pallas import tpu as pltpu
from jax.sharding import PartitionSpec as P

Q_HEADS = 64
KV_HEADS = 8
GROUP = Q_HEADS // KV_HEADS
HD = 128
PAGE = 128
PAGES_P = 3
PROMPTS_DEV = 3
PROMPT = PAGE * PAGES_P
POOL = PROMPTS_DEV * PROMPT
LAYERS = 2
NEAR = 3
CAP = 2
N_GRP = 32
N_TP = 8

LENGTHS_AT = PROMPTS_DEV * PAGES_P
TARGETS_AT = LENGTHS_AT + PROMPTS_DEV
PLACE_AT = TARGETS_AT + PROMPTS_DEV
PLAN_ROWS = 32
HELD_ROWS = 16
CUTS = 6
UNIT = PROMPT + HELD_ROWS

masked_score = -1e30
EXP2_SCALE = math.log2(math.e) / math.sqrt(HD)
VMEM_LIMIT = 48 * 1024 * 1024


def rotary_tables():
    halfway = HD // 2
    inverse = np.exp(
        np.arange(halfway, dtype=np.float32) * np.float32(-2.0 * math.log(500000.0) / HD)
    ).astype(np.float32)
    angles = (np.arange(PROMPT + 8, dtype=np.float32)[:, None] * inverse).astype(np.float64)
    cosine = np.cos(angles).astype(np.float32)
    sine = np.sin(angles).astype(np.float32)
    return np.concatenate([cosine, cosine], axis=1), np.concatenate([-sine, sine], axis=1)


def rotated(values, cosine, sine):
    return values * cosine + pltpu.roll(values, HD // 2, 1) * sine


def nt_dot(left, right):
    return lax.dot_general(left, right, (((1,), (1,)), ((), ())), preferred_element_type=jnp.float32)


def picked(plan, target, rank):
    index = jnp.int32(0)
    found = jnp.int32(0)
    before = jnp.int32(0)
    for r in range(PROMPTS_DEV):
        same = (plan[TARGETS_AT + r] == target).astype(jnp.int32)
        hit = same * (before == rank).astype(jnp.int32)
        index = index + hit * r
        found = found + hit
        before = before + same
    return found * plan[LENGTHS_AT + index], [plan[index * PAGES_P + j] for j in range(PAGES_P)]


def attend_kernel(plan, q_hbm, kv_ref, cos_ref, sin_ref, *rest, first, count):
    out_hbm, token, q_buf, out_buf, keys_rot, values_t, q_sem, out_sem = rest[-8:]
    token[0] = 0
    width = GROUP * HD

    def place(i):
        item = first + i
        return item // PROMPTS_DEV, lax.rem(item, PROMPTS_DEV)

    def page_rows(prompt, j):
        return pl.ds(pl.multiple_of(plan[prompt * PAGES_P + j] * PAGE, PAGE), PAGE)

    def q_copy(i, j):
        layer, prompt = place(i)
        source = q_hbm.at[layer, page_rows(prompt, j), :]
        return pltpu.make_async_copy(source, q_buf.at[i, j], q_sem.at[i, j])

    def out_copy(i, j):
        layer, prompt = place(i)
        rows = pl.ds(pl.multiple_of(prompt * PROMPT + j * PAGE, PAGE), PAGE)
        return pltpu.make_async_copy(out_buf.at[i, j], out_hbm.at[layer, rows, :], out_sem.at[i, j])

    for i in range(count):
        for j in range(PAGES_P):
            q_copy(i, j).start()
    values_t[HD:, :] = jnp.ones((16, PROMPT), jnp.bfloat16)

    def body(i, _):
        _, prompt = place(i)
        length = plan[LENGTHS_AT + prompt]
        for j in range(PAGES_P):
            rows = slice(j * PAGE, (j + 1) * PAGE)
            page = kv_ref[page_rows(prompt, j), :]
            keys = rotated(page[:, :HD].astype(jnp.float32), cos_ref[rows, :], sin_ref[rows, :])
            keys_rot[rows, :] = keys.astype(jnp.bfloat16)
            values_t[:HD, rows] = page[:, HD:].astype(jnp.float32).T.astype(jnp.bfloat16)
        for j in range(PAGES_P):
            q_copy(i, j).wait()
            key = lax.broadcasted_iota(jnp.int32, (PAGE, width), 0)
            query = lax.rem(lax.broadcasted_iota(jnp.int32, (PAGE, width), 1), PAGE)
            rows = slice(j * PAGE, (j + 1) * PAGE)
            held = slice(0, (j + 1) * PAGE)
            cosine, sine = cos_ref[rows, :], sin_ref[rows, :]
            heads = []
            for h in range(GROUP):
                head = q_buf[i, j, :, h * HD : (h + 1) * HD].astype(jnp.float32)
                heads.append(rotated(head, cosine, sine).astype(jnp.bfloat16))
            scores = nt_dot(keys_rot[held, :], jnp.concatenate(heads, axis=0))
            blocks = [scores[b * PAGE : (b + 1) * PAGE] for b in range(j)]
            blocks.append(jnp.where(key <= query, scores[rows], masked_score))
            maximum = jnp.max(functools.reduce(jnp.maximum, blocks), axis=0, keepdims=True)
            weights = [
                jnp.exp2((block - maximum) * EXP2_SCALE).astype(jnp.bfloat16) for block in blocks
            ]
            total = jnp.dot(
                values_t[:, held],
                jnp.concatenate(weights, axis=0),
                preferred_element_type=jnp.float32,
            )
            factor = jnp.where(query[:8] + j * PAGE < length, 1.0 / total[HD : HD + 8], 0.0)
            result = total[:HD] * factor[:1]
            for h in range(GROUP):
                lanes = slice(h * HD, (h + 1) * HD)
                out_buf[i, j, :, lanes] = result[:, lanes].T.astype(jnp.bfloat16)
            out_copy(i, j).start()
        return 0

    lax.fori_loop(0, count, body, 0)
    for i in range(count):
        for j in range(PAGES_P):
            out_copy(i, j).wait()


VMEM = pl.BlockSpec(memory_space=pltpu.VMEM)
SMEM = pl.BlockSpec(memory_space=pltpu.SMEM)
ANY = pl.BlockSpec(memory_space=pl.ANY)
HBM = pl.BlockSpec(memory_space=pltpu.HBM)
ORDER = (1, 3, 5, 0, 2, 4)
BRIEF = pl.CostEstimate(flops=1, bytes_accessed=1, transcendentals=0)


def attend(plan, queries, keys_values, cosine, sine, earlier, first, count, after=()):
    operands = [plan, queries, keys_values, cosine, sine, *after]
    in_specs = [SMEM, HBM, VMEM, VMEM, VMEM] + [ANY] * len(after)
    aliases = {}
    if earlier is not None:
        in_specs.append(HBM)
        aliases = {len(operands): 0}
        operands.append(earlier)
    pages = (count, PAGES_P, PAGE, GROUP * HD)
    return pl.pallas_call(
        functools.partial(attend_kernel, first=first, count=count),
        in_specs=in_specs,
        out_specs=[HBM, SMEM],
        scratch_shapes=[
            pltpu.VMEM(pages, jnp.bfloat16),
            pltpu.VMEM(pages, jnp.bfloat16),
            pltpu.VMEM((PROMPT, HD), jnp.bfloat16),
            pltpu.VMEM((HD + 16, PROMPT), jnp.bfloat16),
            pltpu.SemaphoreType.DMA((count, PAGES_P)),
            pltpu.SemaphoreType.DMA((count, PAGES_P)),
        ],
        out_shape=[
            jax.ShapeDtypeStruct(queries.shape, jnp.bfloat16),
            jax.ShapeDtypeStruct((1,), jnp.int32),
        ],
        input_output_aliases=aliases,
        cost_estimate=BRIEF,
        compiler_params=pltpu.CompilerParams(vmem_limit_bytes=VMEM_LIMIT),
        name="attend",
    )(*operands)


def write_unit(out_ref, source, length, pages, cos_ref, sin_ref):
    for j in range(PAGES_P):
        rows = slice(j * PAGE, (j + 1) * PAGE)
        page = source[pl.ds(pl.multiple_of(pages[j] * PAGE, PAGE), PAGE), :]
        inside = lax.broadcasted_iota(jnp.int32, (PAGE, HD), 0) + j * PAGE < length
        keys = rotated(page[:, :HD].astype(jnp.float32), cos_ref[rows, :], sin_ref[rows, :])
        values = page[:, HD:].astype(jnp.float32)
        out_ref[rows, :HD] = jnp.where(inside, keys, 0.0).astype(jnp.bfloat16)
        out_ref[rows, HD:] = jnp.where(inside, values, 0.0).astype(jnp.bfloat16)
    half = length // 2
    lane = lax.broadcasted_iota(jnp.int32, (HELD_ROWS, 2 * HD), 1)
    held = jnp.where(lane < HD, half, length - 2 * half).astype(jnp.float32)
    out_ref[PROMPT:, :] = held.astype(jnp.bfloat16)


def pack_kernel(plan, own_ref, got_ref, cos_ref, sin_ref, after, *refs):
    core = plan[PLACE_AT] // 2
    column = lax.rem(plan[PLACE_AT], 2)
    copy = None
    if len(refs) == 10:
        copy = pltpu.make_async_copy(refs[0], refs[7], refs[9])
        copy.start()
        refs = refs[1:7] + refs[8:]
    local, near_same, near_other, mid_other, far_same, far_other, plan2, _ = refs
    write = functools.partial(write_unit, cos_ref=cos_ref, sin_ref=sin_ref)

    marks = got_ref[POOL:, :HD].astype(jnp.float32)
    numbers = [jnp.max(marks[r : r + 1, :]).astype(jnp.int32) for r in range(18)]
    for r in range(LENGTHS_AT):
        plan2[r] = numbers[r]
    for r in range(PROMPTS_DEV):
        plan2[LENGTHS_AT + r] = 2 * numbers[LENGTHS_AT + r] + numbers[TARGETS_AT + r]
        plan2[TARGETS_AT + r] = numbers[PLACE_AT + r]

    @pl.when(core == 0)
    def _():
        write(near_same, own_ref, *picked(plan, 0, column))
        write(near_other, own_ref, *picked(plan, 0, 1 - column))

    @pl.when(core == 1)
    def _():
        write(near_same, got_ref, *picked(plan2, 0, column))
        write(near_other, got_ref, *picked(plan2, 0, 1 - column))

    write(local, got_ref, *picked(plan2, 1, column))
    write(mid_other, got_ref, *picked(plan2, 1, 1 - column))
    write(far_same, got_ref, *picked(plan2, 2, column))
    write(far_other, got_ref, *picked(plan2, 2, 1 - column))
    if copy is not None:
        copy.wait()

def pack(plan, own, got, cosine, sine, after, kept=()):
    return pl.pallas_call(
        pack_kernel,
        in_specs=[SMEM, VMEM, VMEM, VMEM, VMEM, ANY] + [VMEM] * len(kept),
        out_specs=[VMEM] * (6 + len(kept)),
        out_shape=[jax.ShapeDtypeStruct((UNIT, 2 * HD), jnp.bfloat16)] * (6 + len(kept)),
        scratch_shapes=[pltpu.SMEM((16,), jnp.int32), pltpu.SemaphoreType.DMA],
        cost_estimate=BRIEF,
        compiler_params=pltpu.CompilerParams(vmem_limit_bytes=VMEM_LIMIT),
        name="pack",
    )(plan, own, got, cosine, sine, after, *kept)


def cut_kernel(*refs, layer):
    if layer == 0:
        page_hbm, lengths_hbm, targets_hbm, source, cos_hbm, sin_hbm = refs[:6]
        slab, plan, cos_ref, sin_ref, sem, page_table, lengths, targets, int_sem = refs[-9:]
        ints = [
            pltpu.make_async_copy(page_hbm, page_table, int_sem.at[0]),
            pltpu.make_async_copy(lengths_hbm, lengths, int_sem.at[1]),
            pltpu.make_async_copy(targets_hbm, targets, int_sem.at[2]),
        ]
    else:
        before, source = refs[:2]
        slab, sem = refs[-2:]
        ints = []
    copies = []
    for i in range(CUTS):
        rows = pl.ds(i * (POOL // CUTS), POOL // CUTS)
        copies.append(pltpu.make_async_copy(source.at[layer, rows], slab.at[rows], sem.at[i]))
    if layer == 0:
        copies.append(pltpu.make_async_copy(cos_hbm, cos_ref, sem.at[CUTS]))
        copies.append(pltpu.make_async_copy(sin_hbm, sin_ref, sem.at[CUTS + 1]))
    if layer == 1:
        rows = pl.ds(POOL, PLAN_ROWS)
        copies.append(pltpu.make_async_copy(before.at[rows], slab.at[rows], sem.at[CUTS]))
    for copy in ints + copies:
        copy.start()
    for copy in ints:
        copy.wait()
    if layer == 0:
        for r in range(PROMPTS_DEV):
            for j in range(PAGES_P):
                plan[r * PAGES_P + j] = page_table[r, j]
            plan[LENGTHS_AT + r] = lengths[r]
            plan[TARGETS_AT + r] = targets[r]
        plan[PLACE_AT] = lax.rem(lax.axis_index("grp"), 2) * 2 + lax.rem(lax.axis_index("tp"), 2)
        halves = [plan[LENGTHS_AT + r] // 2 for r in range(PROMPTS_DEV)]
        numbers = [plan[r] for r in range(LENGTHS_AT)] + halves
        numbers += [plan[LENGTHS_AT + r] - 2 * halves[r] for r in range(PROMPTS_DEV)]
        numbers += [plan[TARGETS_AT + r] for r in range(PROMPTS_DEV)]
        row = lax.broadcasted_iota(jnp.int32, (PLAN_ROWS, 2 * HD), 0)
        marks = jnp.zeros((PLAN_ROWS, 2 * HD), jnp.int32)
        for r, number in enumerate(numbers):
            marks = jnp.where(row == r, number, marks)
        slab[POOL:, :] = marks.astype(jnp.float32).astype(jnp.bfloat16)
    for copy in copies:
        copy.wait()


def cut(operands, layer, after=()):
    slab = jax.ShapeDtypeStruct((POOL + PLAN_ROWS, 2 * HD), jnp.bfloat16)
    out_shape, out_specs, scratch = [slab], [VMEM], [pltpu.SemaphoreType.DMA((CUTS + 2,))]
    in_specs = [VMEM, HBM]
    if layer == 0:
        table = jax.ShapeDtypeStruct((PROMPT + 8, HD), jnp.float32)
        out_shape += [jax.ShapeDtypeStruct((16,), jnp.int32), table, table]
        out_specs += [SMEM, VMEM, VMEM]
        scratch += [
            pltpu.SMEM((PROMPTS_DEV, PAGES_P), jnp.int32),
            pltpu.SMEM((PROMPTS_DEV,), jnp.int32),
            pltpu.SMEM((PROMPTS_DEV,), jnp.int32),
            pltpu.SemaphoreType.DMA((3,)),
        ]
        in_specs = [HBM] * 6
    return pl.pallas_call(
        functools.partial(cut_kernel, layer=layer),
        in_specs=in_specs + [ANY] * len(after),
        out_specs=out_specs,
        scratch_shapes=scratch,
        out_shape=out_shape,
        cost_estimate=BRIEF,
        compiler_params=pltpu.CompilerParams(vmem_limit_bytes=VMEM_LIMIT),
        name="cut",
    )(*operands, *after)


def settle_kernel(plan, *refs, layer):
    units, refs = [refs[ORDER.index(i)] for i in range(6)], refs[6:]
    q_ref, kv_ref, cos_ref, sin_ref = refs[:4]
    pool_ref, step_ref, sem = refs[-3:]
    column = lax.rem(plan[PLACE_AT], 2)

    def copy(k, part):
        head = column if part == 0 else 1 - column
        lanes = pl.ds(pl.multiple_of(head * 2 * HD, 2 * HD), 2 * HD)
        source = units[2 * k + part].at[pl.ds(0, PROMPT), :]
        return pltpu.make_async_copy(source, pool_ref.at[k, layer, :, lanes], sem.at[2 * k + part])

    for k in range(NEAR):
        for part in range(2):
            copy(k, part).start()
    position = lax.broadcasted_iota(jnp.int32, cos_ref.shape, 0).astype(jnp.float32)
    token = lax.broadcasted_iota(jnp.int32, (GROUP, PROMPT), 1).astype(jnp.float32)
    scores, own, fresh_values = [], [], []
    for k in range(NEAR):
        held = units[2 * k][PROMPT : PROMPT + 1, :].astype(jnp.float32)
        held = 2.0 * held[:, :HD] + held[:, HD:]
        cosine = jnp.sum(jnp.where(position == held, cos_ref[...], 0.0), axis=0, keepdims=True)
        sine = jnp.sum(jnp.where(position == held, sin_ref[...], 0.0), axis=0, keepdims=True)
        inside = token < jnp.concatenate([held] * PAGES_P, axis=1)
        queries = q_ref[k, layer, :, :].astype(jnp.float32)
        fresh = kv_ref[k, layer, :, :].astype(jnp.float32)
        for part in range(2):
            head = column if part == 0 else 1 - column
            row = jnp.where(head == 0, queries[:1], queries[1:])
            query = jnp.concatenate([row[:, g * HD : (g + 1) * HD] for g in range(GROUP)], axis=0)
            query = rotated(query, cosine, sine).astype(jnp.bfloat16)
            mine = jnp.where(head == 0, fresh[:1], fresh[1:])
            key = jnp.broadcast_to(mine[:, :HD], (8, HD))
            key = rotated(key, cosine, sine).astype(jnp.bfloat16).astype(jnp.float32)
            cached = units[2 * k + part][:PROMPT, :HD]
            scores.append(jnp.where(inside, nt_dot(query, cached), masked_score))
            own.append(jnp.sum(query.astype(jnp.float32) * key, axis=1, keepdims=True))
            fresh_values.append(jnp.broadcast_to(mine[:, HD:], (GROUP, HD)))
    scores = jnp.concatenate(scores, axis=0)
    own = jnp.concatenate(own, axis=0)
    maximum = jnp.maximum(jnp.max(scores, axis=1, keepdims=True), own)
    exponent = jnp.exp2((scores - maximum) * EXP2_SCALE)
    own = jnp.exp2((own - maximum) * EXP2_SCALE)
    factor = 1.0 / (jnp.sum(exponent, axis=1, keepdims=True) + own)
    weights = (exponent * factor).astype(jnp.bfloat16)
    own = (own * factor).astype(jnp.bfloat16).astype(jnp.float32)
    fresh = own * jnp.concatenate(fresh_values, axis=0)
    for k in range(NEAR):
        results = []
        for part in range(2):
            rows = slice((2 * k + part) * GROUP, (2 * k + part + 1) * GROUP)
            cached = units[2 * k + part][:PROMPT, HD:]
            result = jnp.dot(weights[rows], cached, preferred_element_type=jnp.float32)
            result = result + fresh[rows]
            results.append(
                jnp.concatenate([result[g : g + 1, :] for g in range(GROUP)], axis=1)
            )
        low = jnp.where(column == 0, results[0], results[1])
        high = jnp.where(column == 0, results[1], results[0])
        both = jnp.concatenate([low, high], axis=0)
        if layer == 0:
            step_ref[k, :, :] = both
        else:
            step_ref[k, 0, :, :] = refs[4][k, :, :].astype(jnp.bfloat16)
            step_ref[k, 1, :, :] = both.astype(jnp.bfloat16)
    for k in range(NEAR):
        for part in range(2):
            copy(k, part).wait()


def settle(plan, step_queries, step_kv, cosine, sine, units, earlier, layer):
    in_specs = [SMEM] + [VMEM] * 10
    operands = [plan, *(units[i] for i in ORDER), step_queries, step_kv, cosine, sine]
    aliases = {}
    step = jax.ShapeDtypeStruct((NEAR, 2, GROUP * HD), jnp.float32)
    if earlier is not None:
        pool, step_before = earlier
        in_specs += [VMEM, HBM]
        aliases = {len(operands) + 1: 0}
        operands += [step_before, pool]
        step = jax.ShapeDtypeStruct((NEAR, LAYERS, 2, GROUP * HD), jnp.bfloat16)
    return pl.pallas_call(
        functools.partial(settle_kernel, layer=layer),
        in_specs=in_specs,
        out_specs=[HBM, VMEM],
        scratch_shapes=[pltpu.SemaphoreType.DMA((2 * NEAR,))],
        out_shape=[jax.ShapeDtypeStruct((NEAR, LAYERS, PROMPT, 4 * HD), jnp.bfloat16), step],
        input_output_aliases=aliases,
        cost_estimate=BRIEF,
        compiler_params=pltpu.CompilerParams(vmem_limit_bytes=VMEM_LIMIT),
        name="settle",
    )(*operands)


def moved(value, by, flip, only=None):
    pairs = []
    for g in range(N_GRP):
        target = g ^ 1 if by is None else (g + by) % N_GRP
        for t in range(N_TP):
            pairs.append((g * N_TP + t, target * N_TP + (t ^ flip)))
    return lax.ppermute(value, ("grp", "tp"), pairs)


def on_device(
    prompt_queries, prompt_kv, page_table, prompt_lengths, targets, step_queries, step_kv
):
    tables = [jnp.asarray(table) for table in rotary_tables()]
    page_table, prompt_lengths, targets, prompt_queries, prompt_kv, *tables = (
        pltpu.with_memory_space_constraint(value, pltpu.HBM)
        for value in (
            page_table, prompt_lengths, targets.reshape(-1), prompt_queries, prompt_kv, *tables
        )
    )
    slab, plan, cosine, sine = cut([page_table, prompt_lengths, targets, prompt_kv, *tables], 0)
    got = moved(slab, 2, 0)
    out, token = attend(plan, prompt_queries, slab, cosine, sine, None, 0, 2)
    (later_slab,) = cut([slab, prompt_kv], 1, [token])
    later_got = moved(later_slab, 2, 0)
    out, token = attend(plan, prompt_queries, slab, cosine, sine, out, 2, 1, [later_slab])

    local, near_same, near_other, mid_other, far_first, far_other = pack(
        plan, slab, got, cosine, sine, token
    )
    near_other = moved(near_other, None, 1)
    mid_other = moved(mid_other, 0, 1)
    far_other = moved(far_other, 1, 1)
    near_same = moved(near_same, None, 0)
    units = [near_same, near_other, local, mid_other, None, far_other]

    out, token = attend(
        plan, prompt_queries, later_slab, cosine, sine, out, PROMPTS_DEV, PROMPTS_DEV, [local]
    )
    local, near_same, near_other, mid_other, far_same, far_other, far_first = pack(
        plan, later_slab, later_got, cosine, sine, token, [far_first]
    )
    units[4] = moved(far_first, 1, 0)
    near_other = moved(near_other, None, 1)
    mid_other = moved(mid_other, 0, 1)
    far_other = moved(far_other, 1, 1)
    near_same = moved(near_same, None, 0)
    far_same = moved(far_same, 1, 0)
    later_units = [near_same, near_other, local, mid_other, far_same, far_other]
    step = functools.partial(settle, plan, step_queries, step_kv, cosine, sine)
    earlier = step(units, None, 0)
    pool, step = step(later_units, earlier, 1)
    return out, step, pool


def solution(mesh):
    return jax.shard_map(
        on_device,
        mesh=mesh,
        in_specs=(
            P(None, "grp", "tp"),
            P(None, "grp", "tp"),
            P("grp", None),
            P("grp"),
            P("grp", None),
            P("grp", None, "tp", None),
            P("grp", None, "tp", None),
        ),
        out_specs=(P(None, "grp", "tp"), P("grp", None, "tp", None), P("grp", None, None, "tp")),
        check_vma=False,
    )
```

```python
import functools
import math

import jax
import jax.numpy as jnp
import numpy as np
from jax import lax
from jax.experimental import pallas as pl
from jax.experimental.pallas import tpu as pltpu
from jax.sharding import PartitionSpec as P

Q_HEADS = 64
KV_HEADS = 8
GROUP = Q_HEADS // KV_HEADS
HD = 128
PAGE = 128
PAGES_P = 3
PROMPTS_DEV = 3
PROMPT = PAGE * PAGES_P
POOL = PROMPTS_DEV * PROMPT
LAYERS = 2
NEAR = 3
CAP = 2
N_GRP = 32
N_TP = 8

LENGTHS_AT = PROMPTS_DEV * PAGES_P
TARGETS_AT = LENGTHS_AT + PROMPTS_DEV
PLACE_AT = TARGETS_AT + PROMPTS_DEV
PLAN_ROWS = 32
HELD_ROWS = 16
CUTS = 6
UNIT = PROMPT + HELD_ROWS

masked_score = -1e30
EXP2_SCALE = math.log2(math.e) / math.sqrt(HD)
VMEM_LIMIT = 48 * 1024 * 1024


def rotary_tables():
    halfway = HD // 2
    inverse = np.exp(
        np.arange(halfway, dtype=np.float32) * np.float32(-2.0 * math.log(500000.0) / HD)
    ).astype(np.float32)
    angles = (np.arange(PROMPT + 8, dtype=np.float32)[:, None] * inverse).astype(np.float64)
    cosine = np.cos(angles).astype(np.float32)
    sine = np.sin(angles).astype(np.float32)
    return np.concatenate([cosine, cosine], axis=1), np.concatenate([-sine, sine], axis=1)


def rotated(values, cosine, sine):
    return values * cosine + pltpu.roll(values, HD // 2, 1) * sine


def nt_dot(left, right):
    return lax.dot_general(left, right, (((1,), (1,)), ((), ())), preferred_element_type=jnp.float32)


def picked(plan, target, rank):
    index = jnp.int32(0)
    found = jnp.int32(0)
    before = jnp.int32(0)
    for r in range(PROMPTS_DEV):
        same = (plan[TARGETS_AT + r] == target).astype(jnp.int32)
        hit = same * (before == rank).astype(jnp.int32)
        index = index + hit * r
        found = found + hit
        before = before + same
    return found * plan[LENGTHS_AT + index], [plan[index * PAGES_P + j] for j in range(PAGES_P)]


def slab_copies_of(pool, layer, slab, sem):
    copies = []
    for i in range(CUTS):
        rows = pl.ds(i * (POOL // CUTS), POOL // CUTS)
        copies.append(pltpu.make_async_copy(pool.at[layer, rows], slab.at[rows], sem.at[i]))
    return copies


def attend_kernel(plan, q_hbm, *refs, first, count, supply):
    kv_ref, cos_ref, sin_ref = refs[:3]
    out_hbm, mark, q_buf, out_buf, keys_rot, values_t, q_sem, out_sem, slab_sem = refs[-9:]
    slab_copies = []
    if supply:
        slab_copies = slab_copies_of(refs[3], 1, mark, slab_sem)
        rows = pl.ds(POOL, PLAN_ROWS)
        slab_copies.append(pltpu.make_async_copy(kv_ref.at[rows], mark.at[rows], slab_sem.at[CUTS]))
    else:
        mark[0] = 0
    width = GROUP * HD

    def place(i):
        item = first + i
        return item // PROMPTS_DEV, lax.rem(item, PROMPTS_DEV)

    def page_rows(prompt, j):
        return pl.ds(pl.multiple_of(plan[prompt * PAGES_P + j] * PAGE, PAGE), PAGE)

    def q_copy(i, j):
        layer, prompt = place(i)
        source = q_hbm.at[layer, page_rows(prompt, j), :]
        return pltpu.make_async_copy(source, q_buf.at[i, j], q_sem.at[i, j])

    def out_copy(i, j):
        layer, prompt = place(i)
        rows = pl.ds(pl.multiple_of(prompt * PROMPT + j * PAGE, PAGE), PAGE)
        return pltpu.make_async_copy(out_buf.at[i, j], out_hbm.at[layer, rows, :], out_sem.at[i, j])

    for i in range(count):
        for j in range(PAGES_P):
            q_copy(i, j).start()
    for copy in slab_copies:
        copy.start()
    values_t[HD:, :] = jnp.ones((16, PROMPT), jnp.bfloat16)

    def body(source, i, _):
        _, prompt = place(i)
        length = plan[LENGTHS_AT + prompt]
        for j in range(PAGES_P):
            rows = slice(j * PAGE, (j + 1) * PAGE)
            page = source[page_rows(prompt, j), :]
            keys = rotated(page[:, :HD].astype(jnp.float32), cos_ref[rows, :], sin_ref[rows, :])
            keys_rot[rows, :] = keys.astype(jnp.bfloat16)
            values_t[:HD, rows] = page[:, HD:].astype(jnp.float32).T.astype(jnp.bfloat16)
        for j in range(PAGES_P):
            q_copy(i, j).wait()
            key = lax.broadcasted_iota(jnp.int32, (PAGE, width), 0)
            query = lax.rem(lax.broadcasted_iota(jnp.int32, (PAGE, width), 1), PAGE)
            rows = slice(j * PAGE, (j + 1) * PAGE)
            held = slice(0, (j + 1) * PAGE)
            cosine, sine = cos_ref[rows, :], sin_ref[rows, :]
            heads = []
            for h in range(GROUP):
                head = q_buf[i, j, :, h * HD : (h + 1) * HD].astype(jnp.float32)
                heads.append(rotated(head, cosine, sine).astype(jnp.bfloat16))
            scores = nt_dot(keys_rot[held, :], jnp.concatenate(heads, axis=0))
            blocks = [scores[b * PAGE : (b + 1) * PAGE] for b in range(j)]
            blocks.append(jnp.where(key <= query, scores[rows], masked_score))
            maximum = jnp.max(functools.reduce(jnp.maximum, blocks), axis=0, keepdims=True)
            weights = [
                jnp.exp2((block - maximum) * EXP2_SCALE).astype(jnp.bfloat16) for block in blocks
            ]
            total = jnp.dot(
                values_t[:, held],
                jnp.concatenate(weights, axis=0),
                preferred_element_type=jnp.float32,
            )
            factor = jnp.where(query[:8] + j * PAGE < length, 1.0 / total[HD : HD + 8], 0.0)
            result = total[:HD] * factor[:1]
            for h in range(GROUP):
                lanes = slice(h * HD, (h + 1) * HD)
                out_buf[i, j, :, lanes] = result[:, lanes].T.astype(jnp.bfloat16)
            out_copy(i, j).start()
        return 0

    before = min(count, PROMPTS_DEV) if supply else count
    lax.fori_loop(0, before, functools.partial(body, kv_ref), 0)
    for copy in slab_copies:
        copy.wait()
    if before < count:
        lax.fori_loop(before, count, functools.partial(body, mark), 0)
    for i in range(count):
        for j in range(PAGES_P):
            out_copy(i, j).wait()


VMEM = pl.BlockSpec(memory_space=pltpu.VMEM)
SMEM = pl.BlockSpec(memory_space=pltpu.SMEM)
ANY = pl.BlockSpec(memory_space=pl.ANY)
HBM = pl.BlockSpec(memory_space=pltpu.HBM)
ORDER = (1, 3, 5, 0, 2, 4)
BRIEF = pl.CostEstimate(flops=1, bytes_accessed=1, transcendentals=0)


def attend(plan, queries, slab, cosine, sine, first, count, supply=None, earlier=None, after=()):
    operands = [plan, queries, slab, cosine, sine]
    in_specs = [SMEM, HBM, VMEM, VMEM, VMEM]
    mark = jax.ShapeDtypeStruct((1,), jnp.int32)
    if supply is not None:
        operands.append(supply)
        in_specs.append(HBM)
        mark = jax.ShapeDtypeStruct(slab.shape, slab.dtype)
    operands += after
    in_specs += [ANY] * len(after)
    aliases = {}
    if earlier is not None:
        in_specs.append(HBM)
        aliases = {len(operands): 0}
        operands.append(earlier)
    pages = (count, PAGES_P, PAGE, GROUP * HD)
    return pl.pallas_call(
        functools.partial(attend_kernel, first=first, count=count, supply=supply is not None),
        in_specs=in_specs,
        out_specs=[HBM, SMEM if supply is None else VMEM],
        scratch_shapes=[
            pltpu.VMEM(pages, jnp.bfloat16),
            pltpu.VMEM(pages, jnp.bfloat16),
            pltpu.VMEM((PROMPT, HD), jnp.bfloat16),
            pltpu.VMEM((HD + 16, PROMPT), jnp.bfloat16),
            pltpu.SemaphoreType.DMA((count, PAGES_P)),
            pltpu.SemaphoreType.DMA((count, PAGES_P)),
            pltpu.SemaphoreType.DMA((CUTS + 1,)),
        ],
        out_shape=[jax.ShapeDtypeStruct(queries.shape, jnp.bfloat16), mark],
        input_output_aliases=aliases,
        cost_estimate=BRIEF,
        compiler_params=pltpu.CompilerParams(vmem_limit_bytes=VMEM_LIMIT),
        name="attend",
    )(*operands)


def write_unit(out_ref, source, length, pages, cos_ref, sin_ref):
    for j in range(PAGES_P):
        rows = slice(j * PAGE, (j + 1) * PAGE)
        page = source[pl.ds(pl.multiple_of(pages[j] * PAGE, PAGE), PAGE), :]
        inside = lax.broadcasted_iota(jnp.int32, (PAGE, HD), 0) + j * PAGE < length
        keys = rotated(page[:, :HD].astype(jnp.float32), cos_ref[rows, :], sin_ref[rows, :])
        values = page[:, HD:].astype(jnp.float32)
        out_ref[rows, :HD] = jnp.where(inside, keys, 0.0).astype(jnp.bfloat16)
        out_ref[rows, HD:] = jnp.where(inside, values, 0.0).astype(jnp.bfloat16)
    half = length // 2
    lane = lax.broadcasted_iota(jnp.int32, (HELD_ROWS, 2 * HD), 1)
    held = jnp.where(lane < HD, half, length - 2 * half).astype(jnp.float32)
    out_ref[PROMPT:, :] = held.astype(jnp.bfloat16)


def pack_kernel(plan, own_ref, got_ref, cos_ref, sin_ref, after, *refs):
    core = plan[PLACE_AT] // 2
    column = lax.rem(plan[PLACE_AT], 2)
    copy = None
    if len(refs) == 10:
        copy = pltpu.make_async_copy(refs[0], refs[7], refs[9])
        copy.start()
        refs = refs[1:7] + refs[8:]
    local, near_same, near_other, mid_other, far_same, far_other, plan2, _ = refs
    write = functools.partial(write_unit, cos_ref=cos_ref, sin_ref=sin_ref)

    marks = got_ref[POOL:, :HD].astype(jnp.float32)
    numbers = [jnp.max(marks[r : r + 1, :]).astype(jnp.int32) for r in range(18)]
    for r in range(LENGTHS_AT):
        plan2[r] = numbers[r]
    for r in range(PROMPTS_DEV):
        plan2[LENGTHS_AT + r] = 2 * numbers[LENGTHS_AT + r] + numbers[TARGETS_AT + r]
        plan2[TARGETS_AT + r] = numbers[PLACE_AT + r]

    @pl.when(core == 0)
    def _():
        write(near_same, own_ref, *picked(plan, 0, column))
        write(near_other, own_ref, *picked(plan, 0, 1 - column))

    @pl.when(core == 1)
    def _():
        write(near_same, got_ref, *picked(plan2, 0, column))
        write(near_other, got_ref, *picked(plan2, 0, 1 - column))

    write(local, got_ref, *picked(plan2, 1, column))
    write(mid_other, got_ref, *picked(plan2, 1, 1 - column))
    write(far_same, got_ref, *picked(plan2, 2, column))
    write(far_other, got_ref, *picked(plan2, 2, 1 - column))
    if copy is not None:
        copy.wait()

def pack(plan, own, got, cosine, sine, after, kept=()):
    return pl.pallas_call(
        pack_kernel,
        in_specs=[SMEM, VMEM, VMEM, VMEM, VMEM, ANY] + [VMEM] * len(kept),
        out_specs=[VMEM] * (6 + len(kept)),
        out_shape=[jax.ShapeDtypeStruct((UNIT, 2 * HD), jnp.bfloat16)] * (6 + len(kept)),
        scratch_shapes=[pltpu.SMEM((16,), jnp.int32), pltpu.SemaphoreType.DMA],
        cost_estimate=BRIEF,
        compiler_params=pltpu.CompilerParams(vmem_limit_bytes=VMEM_LIMIT),
        name="pack",
    )(plan, own, got, cosine, sine, after, *kept)


def cut_kernel(*refs):
    page_hbm, lengths_hbm, targets_hbm, source, cos_hbm, sin_hbm = refs[:6]
    slab, plan, cos_ref, sin_ref, sem, page_table, lengths, targets, int_sem = refs[6:]
    ints = [
        pltpu.make_async_copy(page_hbm, page_table, int_sem.at[0]),
        pltpu.make_async_copy(lengths_hbm, lengths, int_sem.at[1]),
        pltpu.make_async_copy(targets_hbm, targets, int_sem.at[2]),
    ]
    copies = slab_copies_of(source, 0, slab, sem)
    copies.append(pltpu.make_async_copy(cos_hbm, cos_ref, sem.at[CUTS]))
    copies.append(pltpu.make_async_copy(sin_hbm, sin_ref, sem.at[CUTS + 1]))
    for copy in ints + copies:
        copy.start()
    for copy in ints:
        copy.wait()
    for r in range(PROMPTS_DEV):
        for j in range(PAGES_P):
            plan[r * PAGES_P + j] = page_table[r, j]
        plan[LENGTHS_AT + r] = lengths[r]
        plan[TARGETS_AT + r] = targets[r]
    plan[PLACE_AT] = lax.rem(lax.axis_index("grp"), 2) * 2 + lax.rem(lax.axis_index("tp"), 2)
    halves = [plan[LENGTHS_AT + r] // 2 for r in range(PROMPTS_DEV)]
    numbers = [plan[r] for r in range(LENGTHS_AT)] + halves
    numbers += [plan[LENGTHS_AT + r] - 2 * halves[r] for r in range(PROMPTS_DEV)]
    numbers += [plan[TARGETS_AT + r] for r in range(PROMPTS_DEV)]
    row = lax.broadcasted_iota(jnp.int32, (PLAN_ROWS, 2 * HD), 0)
    marks = jnp.zeros((PLAN_ROWS, 2 * HD), jnp.int32)
    for r, number in enumerate(numbers):
        marks = jnp.where(row == r, number, marks)
    slab[POOL:, :] = marks.astype(jnp.float32).astype(jnp.bfloat16)
    for copy in copies:
        copy.wait()


def cut(*operands):
    table = jax.ShapeDtypeStruct((PROMPT + 8, HD), jnp.float32)
    return pl.pallas_call(
        cut_kernel,
        in_specs=[HBM] * 6,
        out_specs=[VMEM, SMEM, VMEM, VMEM],
        scratch_shapes=[
            pltpu.SemaphoreType.DMA((CUTS + 2,)),
            pltpu.SMEM((PROMPTS_DEV, PAGES_P), jnp.int32),
            pltpu.SMEM((PROMPTS_DEV,), jnp.int32),
            pltpu.SMEM((PROMPTS_DEV,), jnp.int32),
            pltpu.SemaphoreType.DMA((3,)),
        ],
        out_shape=[
            jax.ShapeDtypeStruct((POOL + PLAN_ROWS, 2 * HD), jnp.bfloat16),
            jax.ShapeDtypeStruct((16,), jnp.int32),
            table,
            table,
        ],
        cost_estimate=BRIEF,
        compiler_params=pltpu.CompilerParams(vmem_limit_bytes=VMEM_LIMIT),
        name="cut",
    )(*operands)


def settle_kernel(plan, *refs, layer):
    units, refs = [refs[ORDER.index(i)] for i in range(6)], refs[6:]
    q_ref, kv_ref, cos_ref, sin_ref = refs[:4]
    pool_ref, step_ref, sem = refs[-3:]
    column = lax.rem(plan[PLACE_AT], 2)

    def copy(k, part):
        head = column if part == 0 else 1 - column
        lanes = pl.ds(pl.multiple_of(head * 2 * HD, 2 * HD), 2 * HD)
        source = units[2 * k + part].at[pl.ds(0, PROMPT), :]
        return pltpu.make_async_copy(source, pool_ref.at[k, layer, :, lanes], sem.at[2 * k + part])

    for k in range(NEAR):
        for part in range(2):
            copy(k, part).start()
    position = lax.broadcasted_iota(jnp.int32, cos_ref.shape, 0).astype(jnp.float32)
    token = lax.broadcasted_iota(jnp.int32, (GROUP, PROMPT), 1).astype(jnp.float32)
    scores, own, fresh_values = [], [], []
    for k in range(NEAR):
        held = units[max(1, 2 * k)][PROMPT : PROMPT + 1, :].astype(jnp.float32)
        held = 2.0 * held[:, :HD] + held[:, HD:]
        cosine = jnp.sum(jnp.where(position == held, cos_ref[...], 0.0), axis=0, keepdims=True)
        sine = jnp.sum(jnp.where(position == held, sin_ref[...], 0.0), axis=0, keepdims=True)
        inside = token < jnp.concatenate([held] * PAGES_P, axis=1)
        queries = q_ref[k, layer, :, :].astype(jnp.float32)
        fresh = kv_ref[k, layer, :, :].astype(jnp.float32)
        for part in range(2):
            head = column if part == 0 else 1 - column
            row = jnp.where(head == 0, queries[:1], queries[1:])
            query = jnp.concatenate([row[:, g * HD : (g + 1) * HD] for g in range(GROUP)], axis=0)
            query = rotated(query, cosine, sine).astype(jnp.bfloat16)
            mine = jnp.where(head == 0, fresh[:1], fresh[1:])
            key = jnp.broadcast_to(mine[:, :HD], (8, HD))
            key = rotated(key, cosine, sine).astype(jnp.bfloat16).astype(jnp.float32)
            cached = units[2 * k + part][:PROMPT, :HD]
            scores.append(jnp.where(inside, nt_dot(query, cached), masked_score))
            own.append(jnp.sum(query.astype(jnp.float32) * key, axis=1, keepdims=True))
            fresh_values.append(jnp.broadcast_to(mine[:, HD:], (GROUP, HD)))
    scores = jnp.concatenate(scores, axis=0)
    own = jnp.concatenate(own, axis=0)
    maximum = jnp.maximum(jnp.max(scores, axis=1, keepdims=True), own)
    exponent = jnp.exp2((scores - maximum) * EXP2_SCALE)
    own = jnp.exp2((own - maximum) * EXP2_SCALE)
    factor = 1.0 / (jnp.sum(exponent, axis=1, keepdims=True) + own)
    weights = (exponent * factor).astype(jnp.bfloat16)
    own = (own * factor).astype(jnp.bfloat16).astype(jnp.float32)
    fresh = own * jnp.concatenate(fresh_values, axis=0)
    for k in range(NEAR):
        results = []
        for part in range(2):
            rows = slice((2 * k + part) * GROUP, (2 * k + part + 1) * GROUP)
            cached = units[2 * k + part][:PROMPT, HD:]
            result = jnp.dot(weights[rows], cached, preferred_element_type=jnp.float32)
            result = result + fresh[rows]
            results.append(
                jnp.concatenate([result[g : g + 1, :] for g in range(GROUP)], axis=1)
            )
        low = jnp.where(column == 0, results[0], results[1])
        high = jnp.where(column == 0, results[1], results[0])
        both = jnp.concatenate([low, high], axis=0)
        if layer == 0:
            step_ref[k, :, :] = both
        else:
            step_ref[k, 0, :, :] = refs[4][k, :, :].astype(jnp.bfloat16)
            step_ref[k, 1, :, :] = both.astype(jnp.bfloat16)
    for k in range(NEAR):
        for part in range(2):
            copy(k, part).wait()


def settle(plan, step_queries, step_kv, cosine, sine, units, earlier, layer):
    in_specs = [SMEM] + [VMEM] * 10
    operands = [plan, *(units[i] for i in ORDER), step_queries, step_kv, cosine, sine]
    aliases = {}
    step = jax.ShapeDtypeStruct((NEAR, 2, GROUP * HD), jnp.float32)
    if earlier is not None:
        pool, step_before = earlier
        in_specs += [VMEM, HBM]
        aliases = {len(operands) + 1: 0}
        operands += [step_before, pool]
        step = jax.ShapeDtypeStruct((NEAR, LAYERS, 2, GROUP * HD), jnp.bfloat16)
    return pl.pallas_call(
        functools.partial(settle_kernel, layer=layer),
        in_specs=in_specs,
        out_specs=[HBM, VMEM],
        scratch_shapes=[pltpu.SemaphoreType.DMA((2 * NEAR,))],
        out_shape=[jax.ShapeDtypeStruct((NEAR, LAYERS, PROMPT, 4 * HD), jnp.bfloat16), step],
        input_output_aliases=aliases,
        cost_estimate=BRIEF,
        compiler_params=pltpu.CompilerParams(vmem_limit_bytes=VMEM_LIMIT),
        name="settle",
    )(*operands)


def moved(value, by, flip, only=None):
    pairs = []
    for g in range(N_GRP):
        target = g ^ 1 if by is None else (g + by) % N_GRP
        for t in range(N_TP):
            pairs.append((g * N_TP + t, target * N_TP + (t ^ flip)))
    return lax.ppermute(value, ("grp", "tp"), pairs)


def on_device(
    prompt_queries, prompt_kv, page_table, prompt_lengths, targets, step_queries, step_kv
):
    tables = [jnp.asarray(table) for table in rotary_tables()]
    page_table, prompt_lengths, targets, prompt_queries, prompt_kv, *tables = (
        pltpu.with_memory_space_constraint(value, pltpu.HBM)
        for value in (
            page_table, prompt_lengths, targets.reshape(-1), prompt_queries, prompt_kv, *tables
        )
    )
    slab, plan, cosine, sine = cut(page_table, prompt_lengths, targets, prompt_kv, *tables)
    got = moved(slab, 2, 0)
    attention = functools.partial(attend, plan, prompt_queries)
    out, later_slab = attention(slab, cosine, sine, 0, 4, prompt_kv)
    later_got = moved(later_slab, 2, 0)

    local, near_first, near_other, mid_other, far_same, far_other = pack(
        plan, slab, got, cosine, sine, later_slab
    )
    near_other = moved(near_other, None, 1)
    mid_other = moved(mid_other, 0, 1)
    far_other = moved(far_other, 1, 1)
    far_same = moved(far_same, 1, 0)
    units = [None, near_other, local, mid_other, far_same, far_other]

    out, mark = attention(later_slab, cosine, sine, 4, 2, None, out, [local])
    local, near_same, near_other, mid_other, far_same, far_other, near_first = pack(
        plan, later_slab, later_got, cosine, sine, mark, [near_first]
    )
    units[0] = moved(near_first, None, 0)
    near_other = moved(near_other, None, 1)
    mid_other = moved(mid_other, 0, 1)
    far_other = moved(far_other, 1, 1)
    near_same = moved(near_same, None, 0)
    far_same = moved(far_same, 1, 0)
    later_units = [near_same, near_other, local, mid_other, far_same, far_other]
    step = functools.partial(settle, plan, step_queries, step_kv, cosine, sine)
    earlier = step(units, None, 0)
    pool, step = step(later_units, earlier, 1)
    return out, step, pool


def solution(mesh):
    return jax.shard_map(
        on_device,
        mesh=mesh,
        in_specs=(
            P(None, "grp", "tp"),
            P(None, "grp", "tp"),
            P("grp", None),
            P("grp"),
            P("grp", None),
            P("grp", None, "tp", None),
            P("grp", None, "tp", None),
        ),
        out_specs=(P(None, "grp", "tp"), P("grp", None, "tp", None), P("grp", None, None, "tp")),
        check_vma=False,
    )
```

```python
import functools
import math

import jax
import jax.numpy as jnp
import numpy as np
from jax import lax
from jax.experimental import pallas as pl
from jax.experimental.pallas import tpu as pltpu
from jax.sharding import PartitionSpec as P

Q_HEADS = 64
KV_HEADS = 8
GROUP = Q_HEADS // KV_HEADS
HD = 128
PAGE = 128
PAGES_P = 3
PROMPTS_DEV = 3
PROMPT = PAGE * PAGES_P
POOL = PROMPTS_DEV * PROMPT
LAYERS = 2
NEAR = 3
CAP = 2
N_GRP = 32
N_TP = 8

LENGTHS_AT = PROMPTS_DEV * PAGES_P
TARGETS_AT = LENGTHS_AT + PROMPTS_DEV
PLACE_AT = TARGETS_AT + PROMPTS_DEV
PLAN_ROWS = 32
HELD_ROWS = 16
CUTS = 6
UNIT = PROMPT + HELD_ROWS

masked_score = -1e30
EXP2_SCALE = math.log2(math.e) / math.sqrt(HD)
VMEM_LIMIT = 48 * 1024 * 1024


def rotary_tables():
    halfway = HD // 2
    inverse = np.exp(
        np.arange(halfway, dtype=np.float32) * np.float32(-2.0 * math.log(500000.0) / HD)
    ).astype(np.float32)
    angles = (np.arange(PROMPT + 8, dtype=np.float32)[:, None] * inverse).astype(np.float64)
    cosine = np.cos(angles).astype(np.float32)
    sine = np.sin(angles).astype(np.float32)
    return np.concatenate([cosine, cosine], axis=1), np.concatenate([-sine, sine], axis=1)


def rotated(values, cosine, sine):
    return values * cosine + pltpu.roll(values, HD // 2, 1) * sine


def nt_dot(left, right):
    return lax.dot_general(left, right, (((1,), (1,)), ((), ())), preferred_element_type=jnp.float32)


def picked(plan, target, rank):
    index = jnp.int32(0)
    found = jnp.int32(0)
    before = jnp.int32(0)
    for r in range(PROMPTS_DEV):
        same = (plan[TARGETS_AT + r] == target).astype(jnp.int32)
        hit = same * (before == rank).astype(jnp.int32)
        index = index + hit * r
        found = found + hit
        before = before + same
    return found * plan[LENGTHS_AT + index], [plan[index * PAGES_P + j] for j in range(PAGES_P)]


def slab_copies_of(pool, layer, slab, sem):
    copies = []
    for i in range(CUTS):
        rows = pl.ds(i * (POOL // CUTS), POOL // CUTS)
        copies.append(pltpu.make_async_copy(pool.at[layer, rows], slab.at[rows], sem.at[i]))
    return copies


def attend_kernel(plan, q_hbm, *refs, first, count, supply):
    kv_ref, cos_ref, sin_ref = refs[:3]
    out_hbm, mark, q_buf, out_buf, keys_rot, values_t, q_sem, out_sem, slab_sem = refs[-9:]
    slab_copies = []
    if supply:
        slab_copies = slab_copies_of(refs[3], 1, mark, slab_sem)
        rows = pl.ds(POOL, PLAN_ROWS)
        slab_copies.append(pltpu.make_async_copy(kv_ref.at[rows], mark.at[rows], slab_sem.at[CUTS]))
    else:
        mark[0] = 0
    width = GROUP * HD

    def place(i):
        item = first + i
        return item // PROMPTS_DEV, lax.rem(item, PROMPTS_DEV)

    def page_rows(prompt, j):
        return pl.ds(pl.multiple_of(plan[prompt * PAGES_P + j] * PAGE, PAGE), PAGE)

    def q_copy(i, j):
        layer, prompt = place(i)
        source = q_hbm.at[layer, page_rows(prompt, j), :]
        return pltpu.make_async_copy(source, q_buf.at[i, j], q_sem.at[i, j])

    def out_copy(i, j):
        layer, prompt = place(i)
        rows = pl.ds(pl.multiple_of(prompt * PROMPT + j * PAGE, PAGE), PAGE)
        return pltpu.make_async_copy(out_buf.at[i, j], out_hbm.at[layer, rows, :], out_sem.at[i, j])

    for i in range(count):
        for j in range(PAGES_P):
            q_copy(i, j).start()
    for copy in slab_copies:
        copy.start()
    values_t[HD:, :] = jnp.ones((16, PROMPT), jnp.bfloat16)

    def body(source, i, _):
        _, prompt = place(i)
        length = plan[LENGTHS_AT + prompt]
        for j in range(PAGES_P):
            rows = slice(j * PAGE, (j + 1) * PAGE)
            page = source[page_rows(prompt, j), :]
            keys = rotated(page[:, :HD].astype(jnp.float32), cos_ref[rows, :], sin_ref[rows, :])
            keys_rot[rows, :] = keys.astype(jnp.bfloat16)
            values_t[:HD, rows] = page[:, HD:].astype(jnp.float32).T.astype(jnp.bfloat16)
        for j in range(PAGES_P):
            q_copy(i, j).wait()
            key = lax.broadcasted_iota(jnp.int32, (PAGE, width), 0)
            query = lax.rem(lax.broadcasted_iota(jnp.int32, (PAGE, width), 1), PAGE)
            rows = slice(j * PAGE, (j + 1) * PAGE)
            held = slice(0, (j + 1) * PAGE)
            cosine, sine = cos_ref[rows, :], sin_ref[rows, :]
            heads = []
            for h in range(GROUP):
                head = q_buf[i, j, :, h * HD : (h + 1) * HD].astype(jnp.float32)
                heads.append(rotated(head, cosine, sine).astype(jnp.bfloat16))
            scores = nt_dot(keys_rot[held, :], jnp.concatenate(heads, axis=0))
            blocks = [scores[b * PAGE : (b + 1) * PAGE] for b in range(j)]
            blocks.append(jnp.where(key <= query, scores[rows], masked_score))
            maximum = jnp.max(functools.reduce(jnp.maximum, blocks), axis=0, keepdims=True)
            weights = [
                jnp.exp2((block - maximum) * EXP2_SCALE).astype(jnp.bfloat16) for block in blocks
            ]
            total = jnp.dot(
                values_t[:, held],
                jnp.concatenate(weights, axis=0),
                preferred_element_type=jnp.float32,
            )
            factor = jnp.where(query[:8] + j * PAGE < length, 1.0 / total[HD : HD + 8], 0.0)
            result = total[:HD] * factor[:1]
            for h in range(GROUP):
                lanes = slice(h * HD, (h + 1) * HD)
                out_buf[i, j, :, lanes] = result[:, lanes].T.astype(jnp.bfloat16)
            out_copy(i, j).start()
        return 0

    before = min(count, PROMPTS_DEV) if supply else count
    lax.fori_loop(0, before, functools.partial(body, kv_ref), 0)
    for copy in slab_copies:
        copy.wait()
    if before < count:
        lax.fori_loop(before, count, functools.partial(body, mark), 0)
    for i in range(count):
        for j in range(PAGES_P):
            out_copy(i, j).wait()


VMEM = pl.BlockSpec(memory_space=pltpu.VMEM)
SMEM = pl.BlockSpec(memory_space=pltpu.SMEM)
ANY = pl.BlockSpec(memory_space=pl.ANY)
HBM = pl.BlockSpec(memory_space=pltpu.HBM)
ORDER = (5, 1, 3, 0, 2, 4)
BRIEF = pl.CostEstimate(flops=1, bytes_accessed=1, transcendentals=0)


def attend(plan, queries, slab, cosine, sine, first, count, supply=None, earlier=None, after=()):
    operands = [plan, queries, slab, cosine, sine]
    in_specs = [SMEM, HBM, VMEM, VMEM, VMEM]
    mark = jax.ShapeDtypeStruct((1,), jnp.int32)
    if supply is not None:
        operands.append(supply)
        in_specs.append(HBM)
        mark = jax.ShapeDtypeStruct(slab.shape, slab.dtype)
    operands += after
    in_specs += [ANY] * len(after)
    aliases = {}
    if earlier is not None:
        in_specs.append(HBM)
        aliases = {len(operands): 0}
        operands.append(earlier)
    pages = (count, PAGES_P, PAGE, GROUP * HD)
    return pl.pallas_call(
        functools.partial(attend_kernel, first=first, count=count, supply=supply is not None),
        in_specs=in_specs,
        out_specs=[HBM, SMEM if supply is None else VMEM],
        scratch_shapes=[
            pltpu.VMEM(pages, jnp.bfloat16),
            pltpu.VMEM(pages, jnp.bfloat16),
            pltpu.VMEM((PROMPT, HD), jnp.bfloat16),
            pltpu.VMEM((HD + 16, PROMPT), jnp.bfloat16),
            pltpu.SemaphoreType.DMA((count, PAGES_P)),
            pltpu.SemaphoreType.DMA((count, PAGES_P)),
            pltpu.SemaphoreType.DMA((CUTS + 1,)),
        ],
        out_shape=[jax.ShapeDtypeStruct(queries.shape, jnp.bfloat16), mark],
        input_output_aliases=aliases,
        cost_estimate=BRIEF,
        compiler_params=pltpu.CompilerParams(vmem_limit_bytes=VMEM_LIMIT),
        name="attend",
    )(*operands)


def write_unit(out_ref, source, length, pages, cos_ref, sin_ref):
    for j in range(PAGES_P):
        rows = slice(j * PAGE, (j + 1) * PAGE)
        page = source[pl.ds(pl.multiple_of(pages[j] * PAGE, PAGE), PAGE), :]
        inside = lax.broadcasted_iota(jnp.int32, (PAGE, HD), 0) + j * PAGE < length
        keys = rotated(page[:, :HD].astype(jnp.float32), cos_ref[rows, :], sin_ref[rows, :])
        values = page[:, HD:].astype(jnp.float32)
        out_ref[rows, :HD] = jnp.where(inside, keys, 0.0).astype(jnp.bfloat16)
        out_ref[rows, HD:] = jnp.where(inside, values, 0.0).astype(jnp.bfloat16)
    half = length // 2
    lane = lax.broadcasted_iota(jnp.int32, (HELD_ROWS, 2 * HD), 1)
    held = jnp.where(lane < HD, half, length - 2 * half).astype(jnp.float32)
    out_ref[PROMPT:, :] = held.astype(jnp.bfloat16)


def pack_kernel(plan, own_ref, got_ref, cos_ref, sin_ref, after, *refs):
    core = plan[PLACE_AT] // 2
    column = lax.rem(plan[PLACE_AT], 2)
    copy = None
    if len(refs) == 10:
        copy = pltpu.make_async_copy(refs[0], refs[7], refs[9])
        copy.start()
        refs = refs[1:7] + refs[8:]
    local, near_same, near_other, mid_other, far_same, far_other, plan2, _ = refs
    write = functools.partial(write_unit, cos_ref=cos_ref, sin_ref=sin_ref)

    marks = got_ref[POOL:, :HD].astype(jnp.float32)
    numbers = [jnp.max(marks[r : r + 1, :]).astype(jnp.int32) for r in range(18)]
    for r in range(LENGTHS_AT):
        plan2[r] = numbers[r]
    for r in range(PROMPTS_DEV):
        plan2[LENGTHS_AT + r] = 2 * numbers[LENGTHS_AT + r] + numbers[TARGETS_AT + r]
        plan2[TARGETS_AT + r] = numbers[PLACE_AT + r]

    @pl.when(core == 0)
    def _():
        write(near_same, own_ref, *picked(plan, 0, column))
        write(near_other, own_ref, *picked(plan, 0, 1 - column))

    @pl.when(core == 1)
    def _():
        write(near_same, got_ref, *picked(plan2, 0, column))
        write(near_other, got_ref, *picked(plan2, 0, 1 - column))

    write(local, got_ref, *picked(plan2, 1, column))
    write(mid_other, got_ref, *picked(plan2, 1, 1 - column))
    write(far_same, got_ref, *picked(plan2, 2, column))
    write(far_other, got_ref, *picked(plan2, 2, 1 - column))
    if copy is not None:
        copy.wait()

def pack(plan, own, got, cosine, sine, after, kept=()):
    return pl.pallas_call(
        pack_kernel,
        in_specs=[SMEM, VMEM, VMEM, VMEM, VMEM, ANY] + [VMEM] * len(kept),
        out_specs=[VMEM] * (6 + len(kept)),
        out_shape=[jax.ShapeDtypeStruct((UNIT, 2 * HD), jnp.bfloat16)] * (6 + len(kept)),
        scratch_shapes=[pltpu.SMEM((16,), jnp.int32), pltpu.SemaphoreType.DMA],
        cost_estimate=BRIEF,
        compiler_params=pltpu.CompilerParams(vmem_limit_bytes=VMEM_LIMIT),
        name="pack",
    )(plan, own, got, cosine, sine, after, *kept)


def cut_kernel(*refs):
    page_hbm, lengths_hbm, targets_hbm, source, cos_hbm, sin_hbm = refs[:6]
    slab, plan, cos_ref, sin_ref, sem, page_table, lengths, targets, int_sem = refs[6:]
    ints = [
        pltpu.make_async_copy(page_hbm, page_table, int_sem.at[0]),
        pltpu.make_async_copy(lengths_hbm, lengths, int_sem.at[1]),
        pltpu.make_async_copy(targets_hbm, targets, int_sem.at[2]),
    ]
    copies = slab_copies_of(source, 0, slab, sem)
    copies.append(pltpu.make_async_copy(cos_hbm, cos_ref, sem.at[CUTS]))
    copies.append(pltpu.make_async_copy(sin_hbm, sin_ref, sem.at[CUTS + 1]))
    for copy in ints + copies:
        copy.start()
    for copy in ints:
        copy.wait()
    for r in range(PROMPTS_DEV):
        for j in range(PAGES_P):
            plan[r * PAGES_P + j] = page_table[r, j]
        plan[LENGTHS_AT + r] = lengths[r]
        plan[TARGETS_AT + r] = targets[r]
    plan[PLACE_AT] = lax.rem(lax.axis_index("grp"), 2) * 2 + lax.rem(lax.axis_index("tp"), 2)
    halves = [plan[LENGTHS_AT + r] // 2 for r in range(PROMPTS_DEV)]
    numbers = [plan[r] for r in range(LENGTHS_AT)] + halves
    numbers += [plan[LENGTHS_AT + r] - 2 * halves[r] for r in range(PROMPTS_DEV)]
    numbers += [plan[TARGETS_AT + r] for r in range(PROMPTS_DEV)]
    row = lax.broadcasted_iota(jnp.int32, (PLAN_ROWS, 2 * HD), 0)
    marks = jnp.zeros((PLAN_ROWS, 2 * HD), jnp.int32)
    for r, number in enumerate(numbers):
        marks = jnp.where(row == r, number, marks)
    slab[POOL:, :] = marks.astype(jnp.float32).astype(jnp.bfloat16)
    for copy in copies:
        copy.wait()


def cut(*operands):
    table = jax.ShapeDtypeStruct((PROMPT + 8, HD), jnp.float32)
    return pl.pallas_call(
        cut_kernel,
        in_specs=[HBM] * 6,
        out_specs=[VMEM, SMEM, VMEM, VMEM],
        scratch_shapes=[
            pltpu.SemaphoreType.DMA((CUTS + 2,)),
            pltpu.SMEM((PROMPTS_DEV, PAGES_P), jnp.int32),
            pltpu.SMEM((PROMPTS_DEV,), jnp.int32),
            pltpu.SMEM((PROMPTS_DEV,), jnp.int32),
            pltpu.SemaphoreType.DMA((3,)),
        ],
        out_shape=[
            jax.ShapeDtypeStruct((POOL + PLAN_ROWS, 2 * HD), jnp.bfloat16),
            jax.ShapeDtypeStruct((16,), jnp.int32),
            table,
            table,
        ],
        cost_estimate=BRIEF,
        compiler_params=pltpu.CompilerParams(vmem_limit_bytes=VMEM_LIMIT),
        name="cut",
    )(*operands)


def settle_kernel(*refs, layer):
    units, refs = [refs[ORDER.index(i)] for i in range(6)], refs[6:]
    q_ref, kv_ref, cos_ref, sin_ref = refs[:4]
    pool_ref, step_ref, sem = refs[-3:]
    column = lax.rem(lax.axis_index("tp"), 2)

    def copy(k, part):
        head = column if part == 0 else 1 - column
        lanes = pl.ds(pl.multiple_of(head * 2 * HD, 2 * HD), 2 * HD)
        source = units[2 * k + part].at[pl.ds(0, PROMPT), :]
        return pltpu.make_async_copy(source, pool_ref.at[k, layer, :, lanes], sem.at[2 * k + part])

    for k in range(NEAR):
        for part in range(2):
            copy(k, part).start()
    position = lax.broadcasted_iota(jnp.int32, cos_ref.shape, 0).astype(jnp.float32)
    token = lax.broadcasted_iota(jnp.int32, (GROUP, PROMPT), 1).astype(jnp.float32)
    scores, own, fresh_values = [], [], []
    for k in range(NEAR):
        held = units[max(1, 2 * k)][PROMPT : PROMPT + 1, :].astype(jnp.float32)
        held = 2.0 * held[:, :HD] + held[:, HD:]
        cosine = jnp.sum(jnp.where(position == held, cos_ref[...], 0.0), axis=0, keepdims=True)
        sine = jnp.sum(jnp.where(position == held, sin_ref[...], 0.0), axis=0, keepdims=True)
        inside = token < jnp.concatenate([held] * PAGES_P, axis=1)
        queries = q_ref[k, layer, :, :].astype(jnp.float32)
        fresh = kv_ref[k, layer, :, :].astype(jnp.float32)
        for part in range(2):
            head = column if part == 0 else 1 - column
            row = jnp.where(head == 0, queries[:1], queries[1:])
            query = jnp.concatenate([row[:, g * HD : (g + 1) * HD] for g in range(GROUP)], axis=0)
            query = rotated(query, cosine, sine).astype(jnp.bfloat16)
            mine = jnp.where(head == 0, fresh[:1], fresh[1:])
            key = jnp.broadcast_to(mine[:, :HD], (8, HD))
            key = rotated(key, cosine, sine).astype(jnp.bfloat16).astype(jnp.float32)
            cached = units[2 * k + part][:PROMPT, :HD]
            scores.append(jnp.where(inside, nt_dot(query, cached), masked_score))
            own.append(jnp.sum(query.astype(jnp.float32) * key, axis=1, keepdims=True))
            fresh_values.append(jnp.broadcast_to(mine[:, HD:], (GROUP, HD)))
    scores = jnp.concatenate(scores, axis=0)
    own = jnp.concatenate(own, axis=0)
    maximum = jnp.maximum(jnp.max(scores, axis=1, keepdims=True), own)
    exponent = jnp.exp2((scores - maximum) * EXP2_SCALE)
    own = jnp.exp2((own - maximum) * EXP2_SCALE)
    factor = 1.0 / (jnp.sum(exponent, axis=1, keepdims=True) + own)
    weights = (exponent * factor).astype(jnp.bfloat16)
    own = (own * factor).astype(jnp.bfloat16).astype(jnp.float32)
    fresh = own * jnp.concatenate(fresh_values, axis=0)
    for k in range(NEAR):
        results = []
        for part in range(2):
            rows = slice((2 * k + part) * GROUP, (2 * k + part + 1) * GROUP)
            cached = units[2 * k + part][:PROMPT, HD:]
            result = jnp.dot(weights[rows], cached, preferred_element_type=jnp.float32)
            result = result + fresh[rows]
            results.append(
                jnp.concatenate([result[g : g + 1, :] for g in range(GROUP)], axis=1)
            )
        low = jnp.where(column == 0, results[0], results[1])
        high = jnp.where(column == 0, results[1], results[0])
        both = jnp.concatenate([low, high], axis=0)
        if layer == 0:
            step_ref[k, :, :] = both
        else:
            step_ref[k, 0, :, :] = refs[4][k, :, :].astype(jnp.bfloat16)
            step_ref[k, 1, :, :] = both.astype(jnp.bfloat16)
    for k in range(NEAR):
        for part in range(2):
            copy(k, part).wait()


def settle(step_queries, step_kv, cosine, sine, units, earlier, layer):
    in_specs = [VMEM] * 10
    operands = [*(units[i] for i in ORDER), step_queries, step_kv, cosine, sine]
    aliases = {}
    step = jax.ShapeDtypeStruct((NEAR, 2, GROUP * HD), jnp.float32)
    if earlier is not None:
        pool, step_before = earlier
        in_specs += [VMEM, HBM]
        aliases = {len(operands) + 1: 0}
        operands += [step_before, pool]
        step = jax.ShapeDtypeStruct((NEAR, LAYERS, 2, GROUP * HD), jnp.bfloat16)
    return pl.pallas_call(
        functools.partial(settle_kernel, layer=layer),
        in_specs=in_specs,
        out_specs=[HBM, VMEM],
        scratch_shapes=[pltpu.SemaphoreType.DMA((2 * NEAR,))],
        out_shape=[jax.ShapeDtypeStruct((NEAR, LAYERS, PROMPT, 4 * HD), jnp.bfloat16), step],
        input_output_aliases=aliases,
        cost_estimate=BRIEF,
        compiler_params=pltpu.CompilerParams(vmem_limit_bytes=VMEM_LIMIT),
        name="settle",
    )(*operands)


def moved(value, by, flip, only=None):
    pairs = []
    for g in range(N_GRP):
        target = g ^ 1 if by is None else (g + by) % N_GRP
        for t in range(N_TP):
            pairs.append((g * N_TP + t, target * N_TP + (t ^ flip)))
    return lax.ppermute(value, ("grp", "tp"), pairs)


def on_device(
    prompt_queries, prompt_kv, page_table, prompt_lengths, targets, step_queries, step_kv
):
    tables = [jnp.asarray(table) for table in rotary_tables()]
    page_table, prompt_lengths, targets, prompt_queries, prompt_kv, *tables = (
        pltpu.with_memory_space_constraint(value, pltpu.HBM)
        for value in (
            page_table, prompt_lengths, targets.reshape(-1), prompt_queries, prompt_kv, *tables
        )
    )
    slab, plan, cosine, sine = cut(page_table, prompt_lengths, targets, prompt_kv, *tables)
    got = moved(slab, 2, 0)
    attention = functools.partial(attend, plan, prompt_queries)
    out, later_slab = attention(slab, cosine, sine, 0, 4, prompt_kv)
    later_got = moved(later_slab, 2, 0)

    local, near_first, near_other, mid_other, far_same, far_other = pack(
        plan, slab, got, cosine, sine, later_slab
    )
    far_other = moved(far_other, 1, 1)
    near_other = moved(near_other, None, 1)
    mid_other = moved(mid_other, 0, 1)
    far_same = moved(far_same, 1, 0)
    units = [None, near_other, local, mid_other, far_same, far_other]

    out, mark = attention(later_slab, cosine, sine, 4, 2, None, out, [local])
    local, near_same, near_other, mid_other, far_same, far_other, near_first = pack(
        plan, later_slab, later_got, cosine, sine, mark, [near_first]
    )
    units[0] = moved(near_first, None, 0)
    far_other = moved(far_other, 1, 1)
    near_other = moved(near_other, None, 1)
    mid_other = moved(mid_other, 0, 1)
    near_same = moved(near_same, None, 0)
    far_same = moved(far_same, 1, 0)
    later_units = [near_same, near_other, local, mid_other, far_same, far_other]
    step = functools.partial(settle, step_queries, step_kv, cosine, sine)
    earlier = step(units, None, 0)
    pool, step = step(later_units, earlier, 1)
    return out, step, pool


def solution(mesh):
    return jax.shard_map(
        on_device,
        mesh=mesh,
        in_specs=(
            P(None, "grp", "tp"),
            P(None, "grp", "tp"),
            P("grp", None),
            P("grp"),
            P("grp", None),
            P("grp", None, "tp", None),
            P("grp", None, "tp", None),
        ),
        out_specs=(P(None, "grp", "tp"), P("grp", None, "tp", None), P("grp", None, None, "tp")),
        check_vma=False,
    )
```

```python
import functools
import math

import jax
import jax.numpy as jnp
import numpy as np
from jax import lax
from jax.experimental import pallas as pl
from jax.experimental.pallas import tpu as pltpu
from jax.sharding import PartitionSpec as P

Q_HEADS = 64
KV_HEADS = 8
GROUP = Q_HEADS // KV_HEADS
HD = 128
PAGE = 128
PAGES_P = 3
PROMPTS_DEV = 3
PROMPT = PAGE * PAGES_P
POOL = PROMPTS_DEV * PROMPT
LAYERS = 2
NEAR = 3
CAP = 2
N_GRP = 32
N_TP = 8

LENGTHS_AT = PROMPTS_DEV * PAGES_P
TARGETS_AT = LENGTHS_AT + PROMPTS_DEV
PLACE_AT = TARGETS_AT + PROMPTS_DEV
PLAN_ROWS = 32
HELD_ROWS = 16
CUTS = 6
UNIT = PROMPT + HELD_ROWS

masked_score = -1e30
EXP2_SCALE = math.log2(math.e) / math.sqrt(HD)
VMEM_LIMIT = 48 * 1024 * 1024


def rotary_tables():
    halfway = HD // 2
    inverse = np.exp(
        np.arange(halfway, dtype=np.float32) * np.float32(-2.0 * math.log(500000.0) / HD)
    ).astype(np.float32)
    angles = (np.arange(PROMPT + 8, dtype=np.float32)[:, None] * inverse).astype(np.float64)
    cosine = np.cos(angles).astype(np.float32)
    sine = np.sin(angles).astype(np.float32)
    return np.concatenate([cosine, cosine], axis=1), np.concatenate([-sine, sine], axis=1)


def rotated(values, cosine, sine):
    return values * cosine + pltpu.roll(values, HD // 2, 1) * sine


def nt_dot(left, right):
    return lax.dot_general(left, right, (((1,), (1,)), ((), ())), preferred_element_type=jnp.float32)


def picked(plan, target, rank):
    index = jnp.int32(0)
    found = jnp.int32(0)
    before = jnp.int32(0)
    for r in range(PROMPTS_DEV):
        same = (plan[TARGETS_AT + r] == target).astype(jnp.int32)
        hit = same * (before == rank).astype(jnp.int32)
        index = index + hit * r
        found = found + hit
        before = before + same
    return found * plan[LENGTHS_AT + index], [plan[index * PAGES_P + j] for j in range(PAGES_P)]


def slab_copies_of(pool, layer, slab, sem):
    copies = []
    for i in range(CUTS):
        rows = pl.ds(i * (POOL // CUTS), POOL // CUTS)
        copies.append(pltpu.make_async_copy(pool.at[layer, rows], slab.at[rows], sem.at[i]))
    return copies


def attend_kernel(plan, q_hbm, *refs, first, count, supply):
    kv_ref, cos_ref, sin_ref = refs[:3]
    out_hbm, mark, q_buf, out_buf, keys_rot, values_t, q_sem, out_sem, slab_sem = refs[-9:]
    slab_copies = []
    if supply:
        slab_copies = slab_copies_of(refs[3], 1, mark, slab_sem)
        rows = pl.ds(POOL, PLAN_ROWS)
        slab_copies.append(pltpu.make_async_copy(kv_ref.at[rows], mark.at[rows], slab_sem.at[CUTS]))
    else:
        mark[...] = jnp.zeros_like(mark)
    width = GROUP * HD

    def place(i):
        item = first + i
        return item // PROMPTS_DEV, lax.rem(item, PROMPTS_DEV)

    def page_rows(prompt, j):
        return pl.ds(pl.multiple_of(plan[prompt * PAGES_P + j] * PAGE, PAGE), PAGE)

    def q_copy(i, j):
        layer, prompt = place(i)
        source = q_hbm.at[layer, page_rows(prompt, j), :]
        return pltpu.make_async_copy(source, q_buf.at[i, j], q_sem.at[i, j])

    def out_copy(i, j):
        layer, prompt = place(i)
        rows = pl.ds(pl.multiple_of(prompt * PROMPT + j * PAGE, PAGE), PAGE)
        return pltpu.make_async_copy(out_buf.at[i, j], out_hbm.at[layer, rows, :], out_sem.at[i, j])

    for i in range(count):
        for j in range(PAGES_P):
            q_copy(i, j).start()
    for copy in slab_copies:
        copy.start()
    values_t[HD:, :] = jnp.ones((16, PROMPT), jnp.bfloat16)

    def body(source, i, _):
        _, prompt = place(i)
        length = plan[LENGTHS_AT + prompt]
        for j in range(PAGES_P):
            rows = slice(j * PAGE, (j + 1) * PAGE)
            page = source[page_rows(prompt, j), :]
            keys = rotated(page[:, :HD].astype(jnp.float32), cos_ref[rows, :], sin_ref[rows, :])
            keys_rot[rows, :] = keys.astype(jnp.bfloat16)
            values_t[:HD, rows] = page[:, HD:].astype(jnp.float32).T.astype(jnp.bfloat16)
        for j in range(PAGES_P):
            q_copy(i, j).wait()
            key = lax.broadcasted_iota(jnp.int32, (PAGE, width), 0)
            query = lax.rem(lax.broadcasted_iota(jnp.int32, (PAGE, width), 1), PAGE)
            rows = slice(j * PAGE, (j + 1) * PAGE)
            held = slice(0, (j + 1) * PAGE)
            cosine, sine = cos_ref[rows, :], sin_ref[rows, :]
            heads = []
            for h in range(GROUP):
                head = q_buf[i, j, :, h * HD : (h + 1) * HD].astype(jnp.float32)
                heads.append(rotated(head, cosine, sine).astype(jnp.bfloat16))
            scores = nt_dot(keys_rot[held, :], jnp.concatenate(heads, axis=0))
            blocks = [scores[b * PAGE : (b + 1) * PAGE] for b in range(j)]
            blocks.append(jnp.where(key <= query, scores[rows], masked_score))
            maximum = jnp.max(functools.reduce(jnp.maximum, blocks), axis=0, keepdims=True)
            weights = [
                jnp.exp2((block - maximum) * EXP2_SCALE).astype(jnp.bfloat16) for block in blocks
            ]
            total = jnp.dot(
                values_t[:, held],
                jnp.concatenate(weights, axis=0),
                preferred_element_type=jnp.float32,
            )
            factor = jnp.where(query[:8] + j * PAGE < length, 1.0 / total[HD : HD + 8], 0.0)
            result = total[:HD] * factor[:1]
            for h in range(GROUP):
                lanes = slice(h * HD, (h + 1) * HD)
                out_buf[i, j, :, lanes] = result[:, lanes].T.astype(jnp.bfloat16)
            out_copy(i, j).start()
        return 0

    before = min(count, PROMPTS_DEV) if supply else count
    lax.fori_loop(0, before, functools.partial(body, kv_ref), 0)
    for copy in slab_copies:
        copy.wait()
    if before < count:
        lax.fori_loop(before, count, functools.partial(body, mark), 0)
    for i in range(count):
        for j in range(PAGES_P):
            out_copy(i, j).wait()


VMEM = pl.BlockSpec(memory_space=pltpu.VMEM)
SMEM = pl.BlockSpec(memory_space=pltpu.SMEM)
ANY = pl.BlockSpec(memory_space=pl.ANY)
HBM = pl.BlockSpec(memory_space=pltpu.HBM)
ORDER = (5, 1, 3, 0, 2, 4)
BRIEF = pl.CostEstimate(flops=1, bytes_accessed=1, transcendentals=0)


def attend(plan, queries, slab, cosine, sine, first, count, supply=None, earlier=None, after=()):
    operands = [plan, queries, slab, cosine, sine]
    in_specs = [SMEM, HBM, VMEM, VMEM, VMEM]
    mark = jax.ShapeDtypeStruct((8, HD), jnp.int32)
    if supply is not None:
        operands.append(supply)
        in_specs.append(HBM)
        mark = jax.ShapeDtypeStruct(slab.shape, slab.dtype)
    operands += after
    in_specs += [ANY] * len(after)
    aliases = {}
    if earlier is not None:
        in_specs.append(HBM)
        aliases = {len(operands): 0}
        operands.append(earlier)
    pages = (count, PAGES_P, PAGE, GROUP * HD)
    return pl.pallas_call(
        functools.partial(attend_kernel, first=first, count=count, supply=supply is not None),
        in_specs=in_specs,
        out_specs=[HBM, VMEM],
        scratch_shapes=[
            pltpu.VMEM(pages, jnp.bfloat16),
            pltpu.VMEM(pages, jnp.bfloat16),
            pltpu.VMEM((PROMPT, HD), jnp.bfloat16),
            pltpu.VMEM((HD + 16, PROMPT), jnp.bfloat16),
            pltpu.SemaphoreType.DMA((count, PAGES_P)),
            pltpu.SemaphoreType.DMA((count, PAGES_P)),
            pltpu.SemaphoreType.DMA((CUTS + 1,)),
        ],
        out_shape=[jax.ShapeDtypeStruct(queries.shape, jnp.bfloat16), mark],
        input_output_aliases=aliases,
        cost_estimate=BRIEF,
        compiler_params=pltpu.CompilerParams(vmem_limit_bytes=VMEM_LIMIT),
        name="attend",
    )(*operands)


def write_unit(out_ref, source, length, pages, cos_ref, sin_ref):
    for j in range(PAGES_P):
        rows = slice(j * PAGE, (j + 1) * PAGE)
        page = source[pl.ds(pl.multiple_of(pages[j] * PAGE, PAGE), PAGE), :]
        inside = lax.broadcasted_iota(jnp.int32, (PAGE, HD), 0) + j * PAGE < length
        keys = rotated(page[:, :HD].astype(jnp.float32), cos_ref[rows, :], sin_ref[rows, :])
        values = page[:, HD:].astype(jnp.float32)
        out_ref[rows, :HD] = jnp.where(inside, keys, 0.0).astype(jnp.bfloat16)
        out_ref[rows, HD:] = jnp.where(inside, values, 0.0).astype(jnp.bfloat16)
    half = length // 2
    lane = lax.broadcasted_iota(jnp.int32, (HELD_ROWS, 2 * HD), 1)
    held = jnp.where(lane < HD, half, length - 2 * half).astype(jnp.float32)
    out_ref[PROMPT:, :] = held.astype(jnp.bfloat16)


def pack_kernel(plan_any, own_ref, got_ref, cos_ref, sin_ref, after, *refs):
    plan, plan_sem = refs[-2:]
    refs = refs[:-2]
    plan_copy = pltpu.make_async_copy(plan_any, plan, plan_sem)
    plan_copy.start()
    core = lax.rem(lax.axis_index("grp"), 2)
    column = lax.rem(lax.axis_index("tp"), 2)
    copy = None
    if len(refs) == 10:
        copy = pltpu.make_async_copy(refs[0], refs[7], refs[9])
        copy.start()
        refs = refs[1:7] + refs[8:]
    local, near_same, near_other, mid_other, far_same, far_other, plan2, _ = refs
    write = functools.partial(write_unit, cos_ref=cos_ref, sin_ref=sin_ref)

    marks = got_ref[POOL:, :HD].astype(jnp.float32)
    numbers = [jnp.max(marks[r : r + 1, :]).astype(jnp.int32) for r in range(18)]
    for r in range(LENGTHS_AT):
        plan2[r] = numbers[r]
    for r in range(PROMPTS_DEV):
        plan2[LENGTHS_AT + r] = 2 * numbers[LENGTHS_AT + r] + numbers[TARGETS_AT + r]
        plan2[TARGETS_AT + r] = numbers[PLACE_AT + r]

    write(local, got_ref, *picked(plan2, 1, column))
    write(mid_other, got_ref, *picked(plan2, 1, 1 - column))
    write(far_same, got_ref, *picked(plan2, 2, column))
    write(far_other, got_ref, *picked(plan2, 2, 1 - column))
    plan_copy.wait()

    @pl.when(core == 0)
    def _():
        write(near_same, own_ref, *picked(plan, 0, column))
        write(near_other, own_ref, *picked(plan, 0, 1 - column))

    @pl.when(core == 1)
    def _():
        write(near_same, got_ref, *picked(plan2, 0, column))
        write(near_other, got_ref, *picked(plan2, 0, 1 - column))

    if copy is not None:
        copy.wait()

def pack(plan, own, got, cosine, sine, after, kept=()):
    return pl.pallas_call(
        pack_kernel,
        in_specs=[ANY, VMEM, VMEM, VMEM, VMEM, ANY] + [VMEM] * len(kept),
        out_specs=[VMEM] * (6 + len(kept)),
        out_shape=[jax.ShapeDtypeStruct((UNIT, 2 * HD), jnp.bfloat16)] * (6 + len(kept)),
        scratch_shapes=[
            pltpu.SMEM((16,), jnp.int32),
            pltpu.SemaphoreType.DMA,
            pltpu.SMEM((16,), jnp.int32),
            pltpu.SemaphoreType.DMA,
        ],
        cost_estimate=BRIEF,
        compiler_params=pltpu.CompilerParams(vmem_limit_bytes=VMEM_LIMIT),
        name="pack",
    )(plan, own, got, cosine, sine, after, *kept)


def cut_kernel(*refs):
    page_hbm, lengths_hbm, targets_hbm, source, cos_hbm, sin_hbm = refs[:6]
    slab, plan, cos_ref, sin_ref, sem, page_table, lengths, targets, int_sem = refs[6:]
    ints = [
        pltpu.make_async_copy(page_hbm, page_table, int_sem.at[0]),
        pltpu.make_async_copy(lengths_hbm, lengths, int_sem.at[1]),
        pltpu.make_async_copy(targets_hbm, targets, int_sem.at[2]),
    ]
    copies = slab_copies_of(source, 0, slab, sem)
    copies.append(pltpu.make_async_copy(cos_hbm, cos_ref, sem.at[CUTS]))
    copies.append(pltpu.make_async_copy(sin_hbm, sin_ref, sem.at[CUTS + 1]))
    for copy in ints + copies:
        copy.start()
    for copy in ints:
        copy.wait()
    for r in range(PROMPTS_DEV):
        for j in range(PAGES_P):
            plan[r * PAGES_P + j] = page_table[r, j]
        plan[LENGTHS_AT + r] = lengths[r]
        plan[TARGETS_AT + r] = targets[r]
    plan[PLACE_AT] = lax.rem(lax.axis_index("grp"), 2) * 2 + lax.rem(lax.axis_index("tp"), 2)
    halves = [plan[LENGTHS_AT + r] // 2 for r in range(PROMPTS_DEV)]
    numbers = [plan[r] for r in range(LENGTHS_AT)] + halves
    numbers += [plan[LENGTHS_AT + r] - 2 * halves[r] for r in range(PROMPTS_DEV)]
    numbers += [plan[TARGETS_AT + r] for r in range(PROMPTS_DEV)]
    row = lax.broadcasted_iota(jnp.int32, (PLAN_ROWS, 2 * HD), 0)
    marks = jnp.zeros((PLAN_ROWS, 2 * HD), jnp.int32)
    for r, number in enumerate(numbers):
        marks = jnp.where(row == r, number, marks)
    slab[POOL:, :] = marks.astype(jnp.float32).astype(jnp.bfloat16)
    for copy in copies:
        copy.wait()


def cut(*operands):
    table = jax.ShapeDtypeStruct((PROMPT + 8, HD), jnp.float32)
    return pl.pallas_call(
        cut_kernel,
        in_specs=[HBM] * 6,
        out_specs=[VMEM, SMEM, VMEM, VMEM],
        scratch_shapes=[
            pltpu.SemaphoreType.DMA((CUTS + 2,)),
            pltpu.SMEM((PROMPTS_DEV, PAGES_P), jnp.int32),
            pltpu.SMEM((PROMPTS_DEV,), jnp.int32),
            pltpu.SMEM((PROMPTS_DEV,), jnp.int32),
            pltpu.SemaphoreType.DMA((3,)),
        ],
        out_shape=[
            jax.ShapeDtypeStruct((POOL + PLAN_ROWS, 2 * HD), jnp.bfloat16),
            jax.ShapeDtypeStruct((16,), jnp.int32),
            table,
            table,
        ],
        cost_estimate=BRIEF,
        compiler_params=pltpu.CompilerParams(vmem_limit_bytes=VMEM_LIMIT),
        name="cut",
    )(*operands)


def settle_kernel(*refs, layer):
    units, refs = [refs[ORDER.index(i)] for i in range(6)], refs[6:]
    q_ref, kv_ref, cos_ref, sin_ref = refs[:4]
    pool_ref, step_ref, sem = refs[-3:]
    column = lax.rem(lax.axis_index("tp"), 2)

    def copy(k, part):
        head = column if part == 0 else 1 - column
        lanes = pl.ds(pl.multiple_of(head * 2 * HD, 2 * HD), 2 * HD)
        source = units[2 * k + part].at[pl.ds(0, PROMPT), :]
        return pltpu.make_async_copy(source, pool_ref.at[k, layer, :, lanes], sem.at[2 * k + part])

    for k in range(NEAR):
        for part in range(2):
            copy(k, part).start()
    position = lax.broadcasted_iota(jnp.int32, cos_ref.shape, 0).astype(jnp.float32)
    token = lax.broadcasted_iota(jnp.int32, (GROUP, PROMPT), 1).astype(jnp.float32)
    scores, own, fresh_values = [], [], []
    for k in range(NEAR):
        held = units[max(1, 2 * k)][PROMPT : PROMPT + 1, :].astype(jnp.float32)
        held = 2.0 * held[:, :HD] + held[:, HD:]
        cosine = jnp.sum(jnp.where(position == held, cos_ref[...], 0.0), axis=0, keepdims=True)
        sine = jnp.sum(jnp.where(position == held, sin_ref[...], 0.0), axis=0, keepdims=True)
        inside = token < jnp.concatenate([held] * PAGES_P, axis=1)
        queries = q_ref[k, layer, :, :].astype(jnp.float32)
        fresh = kv_ref[k, layer, :, :].astype(jnp.float32)
        for part in range(2):
            head = column if part == 0 else 1 - column
            row = jnp.where(head == 0, queries[:1], queries[1:])
            query = jnp.concatenate([row[:, g * HD : (g + 1) * HD] for g in range(GROUP)], axis=0)
            query = rotated(query, cosine, sine).astype(jnp.bfloat16)
            mine = jnp.where(head == 0, fresh[:1], fresh[1:])
            key = jnp.broadcast_to(mine[:, :HD], (8, HD))
            key = rotated(key, cosine, sine).astype(jnp.bfloat16).astype(jnp.float32)
            cached = units[2 * k + part][:PROMPT, :HD]
            scores.append(jnp.where(inside, nt_dot(query, cached), masked_score))
            own.append(jnp.sum(query.astype(jnp.float32) * key, axis=1, keepdims=True))
            fresh_values.append(jnp.broadcast_to(mine[:, HD:], (GROUP, HD)))
    scores = jnp.concatenate(scores, axis=0)
    own = jnp.concatenate(own, axis=0)
    maximum = jnp.maximum(jnp.max(scores, axis=1, keepdims=True), own)
    exponent = jnp.exp2((scores - maximum) * EXP2_SCALE)
    own = jnp.exp2((own - maximum) * EXP2_SCALE)
    factor = 1.0 / (jnp.sum(exponent, axis=1, keepdims=True) + own)
    weights = (exponent * factor).astype(jnp.bfloat16)
    own = (own * factor).astype(jnp.bfloat16).astype(jnp.float32)
    fresh = own * jnp.concatenate(fresh_values, axis=0)
    for k in range(NEAR):
        results = []
        for part in range(2):
            rows = slice((2 * k + part) * GROUP, (2 * k + part + 1) * GROUP)
            cached = units[2 * k + part][:PROMPT, HD:]
            result = jnp.dot(weights[rows], cached, preferred_element_type=jnp.float32)
            result = result + fresh[rows]
            results.append(
                jnp.concatenate([result[g : g + 1, :] for g in range(GROUP)], axis=1)
            )
        low = jnp.where(column == 0, results[0], results[1])
        high = jnp.where(column == 0, results[1], results[0])
        both = jnp.concatenate([low, high], axis=0)
        if layer == 0:
            step_ref[k, :, :] = both
        else:
            step_ref[k, 0, :, :] = refs[4][k, :, :].astype(jnp.bfloat16)
            step_ref[k, 1, :, :] = both.astype(jnp.bfloat16)
    for k in range(NEAR):
        for part in range(2):
            copy(k, part).wait()


def settle(step_queries, step_kv, cosine, sine, units, earlier, layer):
    in_specs = [VMEM] * 10
    operands = [*(units[i] for i in ORDER), step_queries, step_kv, cosine, sine]
    aliases = {}
    step = jax.ShapeDtypeStruct((NEAR, 2, GROUP * HD), jnp.float32)
    if earlier is not None:
        pool, step_before = earlier
        in_specs += [VMEM, HBM]
        aliases = {len(operands) + 1: 0}
        operands += [step_before, pool]
        step = jax.ShapeDtypeStruct((NEAR, LAYERS, 2, GROUP * HD), jnp.bfloat16)
    return pl.pallas_call(
        functools.partial(settle_kernel, layer=layer),
        in_specs=in_specs,
        out_specs=[HBM, VMEM],
        scratch_shapes=[pltpu.SemaphoreType.DMA((2 * NEAR,))],
        out_shape=[jax.ShapeDtypeStruct((NEAR, LAYERS, PROMPT, 4 * HD), jnp.bfloat16), step],
        input_output_aliases=aliases,
        cost_estimate=BRIEF,
        compiler_params=pltpu.CompilerParams(vmem_limit_bytes=VMEM_LIMIT),
        name="settle",
    )(*operands)


def moved(value, by, flip, only=None):
    pairs = []
    for g in range(N_GRP):
        target = g ^ 1 if by is None else (g + by) % N_GRP
        for t in range(N_TP):
            pairs.append((g * N_TP + t, target * N_TP + (t ^ flip)))
    return lax.ppermute(value, ("grp", "tp"), pairs)


def on_device(
    prompt_queries, prompt_kv, page_table, prompt_lengths, targets, step_queries, step_kv
):
    tables = [jnp.asarray(table) for table in rotary_tables()]
    page_table, prompt_lengths, targets, prompt_queries, prompt_kv, *tables = (
        pltpu.with_memory_space_constraint(value, pltpu.HBM)
        for value in (
            page_table, prompt_lengths, targets.reshape(-1), prompt_queries, prompt_kv, *tables
        )
    )
    slab, plan, cosine, sine = cut(page_table, prompt_lengths, targets, prompt_kv, *tables)
    got = moved(slab, 2, 0)
    attention = functools.partial(attend, plan, prompt_queries)
    out, later_slab = attention(slab, cosine, sine, 0, 4, prompt_kv)
    later_got = moved(later_slab, 2, 0)

    local, near_first, near_other, mid_other, far_same, far_other = pack(
        plan, slab, got, cosine, sine, later_slab
    )
    far_other = moved(far_other, 1, 1)
    near_other = moved(near_other, None, 1)
    mid_other = moved(mid_other, 0, 1)
    far_same = moved(far_same, 1, 0)
    units = [None, near_other, local, mid_other, far_same, far_other]

    out, mark = attention(later_slab, cosine, sine, 4, 2, None, out, [local])
    local, near_same, near_other, mid_other, far_same, far_other, near_first = pack(
        plan, later_slab, later_got, cosine, sine, mark, [near_first]
    )
    units[0] = moved(near_first, None, 0)
    far_other = moved(far_other, 1, 1)
    near_other = moved(near_other, None, 1)
    mid_other = moved(mid_other, 0, 1)
    near_same = moved(near_same, None, 0)
    far_same = moved(far_same, 1, 0)
    later_units = [near_same, near_other, local, mid_other, far_same, far_other]
    step = functools.partial(settle, step_queries, step_kv, cosine, sine)
    earlier = step(units, None, 0)
    pool, step = step(later_units, earlier, 1)
    return out, step, pool


def solution(mesh):
    return jax.shard_map(
        on_device,
        mesh=mesh,
        in_specs=(
            P(None, "grp", "tp"),
            P(None, "grp", "tp"),
            P("grp", None),
            P("grp"),
            P("grp", None),
            P("grp", None, "tp", None),
            P("grp", None, "tp", None),
        ),
        out_specs=(P(None, "grp", "tp"), P("grp", None, "tp", None), P("grp", None, None, "tp")),
        check_vma=False,
    )
```

```python
import functools
import math

import jax
import jax.numpy as jnp
import numpy as np
from jax import lax
from jax.experimental import pallas as pl
from jax.experimental.pallas import tpu as pltpu
from jax.sharding import PartitionSpec as P

Q_HEADS = 64
KV_HEADS = 8
GROUP = Q_HEADS // KV_HEADS
HD = 128
PAGE = 128
PAGES_P = 3
PROMPTS_DEV = 3
PROMPT = PAGE * PAGES_P
POOL = PROMPTS_DEV * PROMPT
LAYERS = 2
NEAR = 3
CAP = 2
N_GRP = 32
N_TP = 8

LENGTHS_AT = PROMPTS_DEV * PAGES_P
TARGETS_AT = LENGTHS_AT + PROMPTS_DEV
PLACE_AT = TARGETS_AT + PROMPTS_DEV
PLAN_ROWS = 32
HELD_ROWS = 16
CUTS = 6
UNIT = PROMPT + HELD_ROWS

masked_score = -1e30
EXP2_SCALE = math.log2(math.e) / math.sqrt(HD)
VMEM_LIMIT = 48 * 1024 * 1024


def rotary_tables():
    halfway = HD // 2
    inverse = np.exp(
        np.arange(halfway, dtype=np.float32) * np.float32(-2.0 * math.log(500000.0) / HD)
    ).astype(np.float32)
    angles = (np.arange(PROMPT + 8, dtype=np.float32)[:, None] * inverse).astype(np.float64)
    cosine = np.cos(angles).astype(np.float32)
    sine = np.sin(angles).astype(np.float32)
    return np.concatenate([cosine, cosine], axis=1), np.concatenate([-sine, sine], axis=1)


def rotated(values, cosine, sine):
    return values * cosine + pltpu.roll(values, HD // 2, 1) * sine


def nt_dot(left, right):
    return lax.dot_general(left, right, (((1,), (1,)), ((), ())), preferred_element_type=jnp.float32)


def picked(plan, target, rank):
    index = jnp.int32(0)
    found = jnp.int32(0)
    before = jnp.int32(0)
    for r in range(PROMPTS_DEV):
        same = (plan[TARGETS_AT + r] == target).astype(jnp.int32)
        hit = same * (before == rank).astype(jnp.int32)
        index = index + hit * r
        found = found + hit
        before = before + same
    return found * plan[LENGTHS_AT + index], [plan[index * PAGES_P + j] for j in range(PAGES_P)]


def slab_copies_of(pool, layer, slab, sem):
    copies = []
    for i in range(CUTS):
        rows = pl.ds(i * (POOL // CUTS), POOL // CUTS)
        copies.append(pltpu.make_async_copy(pool.at[layer, rows], slab.at[rows], sem.at[i]))
    return copies


def attend_kernel(plan, q_hbm, *refs, first, count, supply):
    kv_ref, cos_ref, sin_ref = refs[:3]
    out_hbm, mark, q_buf, out_buf, keys_rot, values_t, q_sem, out_sem, slab_sem = refs[-9:]
    slab_copies = []
    if supply:
        slab_copies = slab_copies_of(refs[3], 1, mark, slab_sem)
        rows = pl.ds(POOL, PLAN_ROWS)
        slab_copies.append(pltpu.make_async_copy(kv_ref.at[rows], mark.at[rows], slab_sem.at[CUTS]))
    else:
        mark[...] = jnp.zeros_like(mark)
    width = GROUP * HD

    def place(i):
        item = first + i
        return item // PROMPTS_DEV, lax.rem(item, PROMPTS_DEV)

    def page_rows(prompt, j):
        return pl.ds(pl.multiple_of(plan[prompt * PAGES_P + j] * PAGE, PAGE), PAGE)

    def q_copy(i, j):
        layer, prompt = place(i)
        source = q_hbm.at[layer, page_rows(prompt, j), :]
        return pltpu.make_async_copy(source, q_buf.at[i, j], q_sem.at[i, j])

    def out_copy(i, j):
        layer, prompt = place(i)
        rows = pl.ds(pl.multiple_of(prompt * PROMPT + j * PAGE, PAGE), PAGE)
        return pltpu.make_async_copy(out_buf.at[i, j], out_hbm.at[layer, rows, :], out_sem.at[i, j])

    for i in range(count):
        for j in range(PAGES_P):
            q_copy(i, j).start()
    for copy in slab_copies:
        copy.start()
    values_t[HD:, :] = jnp.ones((16, PROMPT), jnp.bfloat16)

    def body(source, i, _):
        _, prompt = place(i)
        length = plan[LENGTHS_AT + prompt]
        for j in range(PAGES_P):
            rows = slice(j * PAGE, (j + 1) * PAGE)
            page = source[page_rows(prompt, j), :]
            keys = rotated(page[:, :HD].astype(jnp.float32), cos_ref[rows, :], sin_ref[rows, :])
            keys_rot[rows, :] = keys.astype(jnp.bfloat16)
            values_t[:HD, rows] = page[:, HD:].astype(jnp.float32).T.astype(jnp.bfloat16)
        for j in range(PAGES_P):
            q_copy(i, j).wait()
            key = lax.broadcasted_iota(jnp.int32, (PAGE, width), 0)
            query = lax.rem(lax.broadcasted_iota(jnp.int32, (PAGE, width), 1), PAGE)
            rows = slice(j * PAGE, (j + 1) * PAGE)
            held = slice(0, (j + 1) * PAGE)
            cosine, sine = cos_ref[rows, :], sin_ref[rows, :]
            heads = []
            for h in range(GROUP):
                head = q_buf[i, j, :, h * HD : (h + 1) * HD].astype(jnp.float32)
                heads.append(rotated(head, cosine, sine).astype(jnp.bfloat16))
            scores = nt_dot(keys_rot[held, :], jnp.concatenate(heads, axis=0))
            blocks = [scores[b * PAGE : (b + 1) * PAGE] for b in range(j)]
            blocks.append(jnp.where(key <= query, scores[rows], masked_score))
            maximum = jnp.max(functools.reduce(jnp.maximum, blocks), axis=0, keepdims=True)
            weights = [
                jnp.exp2((block - maximum) * EXP2_SCALE).astype(jnp.bfloat16) for block in blocks
            ]
            total = jnp.dot(
                values_t[:, held],
                jnp.concatenate(weights, axis=0),
                preferred_element_type=jnp.float32,
            )
            factor = jnp.where(query[:8] + j * PAGE < length, 1.0 / total[HD : HD + 8], 0.0)
            result = total[:HD] * factor[:1]
            for h in range(GROUP):
                lanes = slice(h * HD, (h + 1) * HD)
                out_buf[i, j, :, lanes] = result[:, lanes].T.astype(jnp.bfloat16)
            out_copy(i, j).start()
        return 0

    before = min(count, PROMPTS_DEV) if supply else count
    lax.fori_loop(0, before, functools.partial(body, kv_ref), 0)
    for copy in slab_copies:
        copy.wait()
    if before < count:
        lax.fori_loop(before, count, functools.partial(body, mark), 0)
    for i in range(count):
        for j in range(PAGES_P):
            out_copy(i, j).wait()


VMEM = pl.BlockSpec(memory_space=pltpu.VMEM)
SMEM = pl.BlockSpec(memory_space=pltpu.SMEM)
ANY = pl.BlockSpec(memory_space=pl.ANY)
HBM = pl.BlockSpec(memory_space=pltpu.HBM)
ORDER = (5, 1, 3, 0, 2, 4)
BRIEF = pl.CostEstimate(flops=1, bytes_accessed=1, transcendentals=0)


def attend(plan, queries, slab, cosine, sine, first, count, supply=None, earlier=None, after=()):
    operands = [plan, queries, slab, cosine, sine]
    in_specs = [SMEM, HBM, VMEM, VMEM, VMEM]
    mark = jax.ShapeDtypeStruct((8, HD), jnp.int32)
    if supply is not None:
        operands.append(supply)
        in_specs.append(HBM)
        mark = jax.ShapeDtypeStruct(slab.shape, slab.dtype)
    operands += after
    in_specs += [ANY] * len(after)
    aliases = {}
    if earlier is not None:
        in_specs.append(HBM)
        aliases = {len(operands): 0}
        operands.append(earlier)
    pages = (count, PAGES_P, PAGE, GROUP * HD)
    return pl.pallas_call(
        functools.partial(attend_kernel, first=first, count=count, supply=supply is not None),
        in_specs=in_specs,
        out_specs=[HBM, VMEM],
        scratch_shapes=[
            pltpu.VMEM(pages, jnp.bfloat16),
            pltpu.VMEM(pages, jnp.bfloat16),
            pltpu.VMEM((PROMPT, HD), jnp.bfloat16),
            pltpu.VMEM((HD + 16, PROMPT), jnp.bfloat16),
            pltpu.SemaphoreType.DMA((count, PAGES_P)),
            pltpu.SemaphoreType.DMA((count, PAGES_P)),
            pltpu.SemaphoreType.DMA((CUTS + 1,)),
        ],
        out_shape=[jax.ShapeDtypeStruct(queries.shape, jnp.bfloat16), mark],
        input_output_aliases=aliases,
        cost_estimate=BRIEF,
        compiler_params=pltpu.CompilerParams(vmem_limit_bytes=VMEM_LIMIT),
        name="attend",
    )(*operands)


def write_unit(out_ref, source, length, pages, cos_ref, sin_ref):
    for j in range(PAGES_P):
        rows = slice(j * PAGE, (j + 1) * PAGE)
        page = source[pl.ds(pl.multiple_of(pages[j] * PAGE, PAGE), PAGE), :]
        inside = lax.broadcasted_iota(jnp.int32, (PAGE, HD), 0) + j * PAGE < length
        keys = rotated(page[:, :HD].astype(jnp.float32), cos_ref[rows, :], sin_ref[rows, :])
        values = page[:, HD:].astype(jnp.float32)
        out_ref[rows, :HD] = jnp.where(inside, keys, 0.0).astype(jnp.bfloat16)
        out_ref[rows, HD:] = jnp.where(inside, values, 0.0).astype(jnp.bfloat16)
    half = length // 2
    lane = lax.broadcasted_iota(jnp.int32, (HELD_ROWS, 2 * HD), 1)
    held = jnp.where(lane < HD, half, length - 2 * half).astype(jnp.float32)
    out_ref[PROMPT:, :] = held.astype(jnp.bfloat16)


def pack_kernel(plan_any, own_ref, got_ref, cos_ref, sin_ref, after, *refs):
    plan, plan_sem = refs[-2:]
    refs = refs[:-2]
    plan_copy = pltpu.make_async_copy(plan_any, plan, plan_sem)
    plan_copy.start()
    core = lax.rem(lax.axis_index("grp"), 2)
    column = lax.rem(lax.axis_index("tp"), 2)
    copy = None
    if len(refs) == 10:
        copy = pltpu.make_async_copy(refs[0], refs[7], refs[9])
        copy.start()
        refs = refs[1:7] + refs[8:]
    local, near_same, near_other, mid_other, far_same, far_other, plan2, _ = refs
    write = functools.partial(write_unit, cos_ref=cos_ref, sin_ref=sin_ref)

    marks = got_ref[POOL:, :HD].astype(jnp.float32)
    numbers = [jnp.max(marks[r : r + 1, :]).astype(jnp.int32) for r in range(18)]
    for r in range(LENGTHS_AT):
        plan2[r] = numbers[r]
    for r in range(PROMPTS_DEV):
        plan2[LENGTHS_AT + r] = 2 * numbers[LENGTHS_AT + r] + numbers[TARGETS_AT + r]
        plan2[TARGETS_AT + r] = numbers[PLACE_AT + r]

    write(local, got_ref, *picked(plan2, 1, column))
    write(mid_other, got_ref, *picked(plan2, 1, 1 - column))
    write(far_same, got_ref, *picked(plan2, 2, column))
    write(far_other, got_ref, *picked(plan2, 2, 1 - column))
    plan_copy.wait()

    @pl.when(core == 0)
    def _():
        write(near_same, own_ref, *picked(plan, 0, column))
        write(near_other, own_ref, *picked(plan, 0, 1 - column))

    @pl.when(core == 1)
    def _():
        write(near_same, got_ref, *picked(plan2, 0, column))
        write(near_other, got_ref, *picked(plan2, 0, 1 - column))

    if copy is not None:
        copy.wait()

def pack(plan, own, got, cosine, sine, after, kept=()):
    return pl.pallas_call(
        pack_kernel,
        in_specs=[ANY, VMEM, VMEM, VMEM, VMEM, ANY] + [VMEM] * len(kept),
        out_specs=[VMEM] * (6 + len(kept)),
        out_shape=[jax.ShapeDtypeStruct((UNIT, 2 * HD), jnp.bfloat16)] * (6 + len(kept)),
        scratch_shapes=[
            pltpu.SMEM((16,), jnp.int32),
            pltpu.SemaphoreType.DMA,
            pltpu.SMEM((16,), jnp.int32),
            pltpu.SemaphoreType.DMA,
        ],
        cost_estimate=BRIEF,
        compiler_params=pltpu.CompilerParams(vmem_limit_bytes=VMEM_LIMIT),
        name="pack",
    )(plan, own, got, cosine, sine, after, *kept)


def cut_kernel(*refs):
    page_hbm, lengths_hbm, targets_hbm, source, cos_hbm, sin_hbm = refs[:6]
    slab, plan_out, cos_ref, sin_ref, sem, page_table, lengths, targets, int_sem, plan = refs[6:]
    ints = [
        pltpu.make_async_copy(page_hbm, page_table, int_sem.at[0]),
        pltpu.make_async_copy(lengths_hbm, lengths, int_sem.at[1]),
        pltpu.make_async_copy(targets_hbm, targets, int_sem.at[2]),
    ]
    copies = slab_copies_of(source, 0, slab, sem)
    copies.append(pltpu.make_async_copy(cos_hbm, cos_ref, sem.at[CUTS]))
    copies.append(pltpu.make_async_copy(sin_hbm, sin_ref, sem.at[CUTS + 1]))
    for copy in ints + copies:
        copy.start()
    for copy in ints:
        copy.wait()
    for r in range(PROMPTS_DEV):
        for j in range(PAGES_P):
            plan[r * PAGES_P + j] = page_table[r, j]
        plan[LENGTHS_AT + r] = lengths[r]
        plan[TARGETS_AT + r] = targets[r]
    plan[PLACE_AT] = lax.rem(lax.axis_index("grp"), 2) * 2 + lax.rem(lax.axis_index("tp"), 2)
    copies.append(pltpu.make_async_copy(plan, plan_out, int_sem.at[3]))
    copies[-1].start()
    halves = [plan[LENGTHS_AT + r] // 2 for r in range(PROMPTS_DEV)]
    numbers = [plan[r] for r in range(LENGTHS_AT)] + halves
    numbers += [plan[LENGTHS_AT + r] - 2 * halves[r] for r in range(PROMPTS_DEV)]
    numbers += [plan[TARGETS_AT + r] for r in range(PROMPTS_DEV)]
    row = lax.broadcasted_iota(jnp.int32, (PLAN_ROWS, 2 * HD), 0)
    marks = jnp.zeros((PLAN_ROWS, 2 * HD), jnp.int32)
    for r, number in enumerate(numbers):
        marks = jnp.where(row == r, number, marks)
    slab[POOL:, :] = marks.astype(jnp.float32).astype(jnp.bfloat16)
    for copy in copies:
        copy.wait()


def cut(*operands):
    table = jax.ShapeDtypeStruct((PROMPT + 8, HD), jnp.float32)
    return pl.pallas_call(
        cut_kernel,
        in_specs=[HBM] * 6,
        out_specs=[VMEM, HBM, VMEM, VMEM],
        scratch_shapes=[
            pltpu.SemaphoreType.DMA((CUTS + 2,)),
            pltpu.SMEM((PROMPTS_DEV, PAGES_P), jnp.int32),
            pltpu.SMEM((PROMPTS_DEV,), jnp.int32),
            pltpu.SMEM((PROMPTS_DEV,), jnp.int32),
            pltpu.SemaphoreType.DMA((4,)),
            pltpu.SMEM((16,), jnp.int32),
        ],
        out_shape=[
            jax.ShapeDtypeStruct((POOL + PLAN_ROWS, 2 * HD), jnp.bfloat16),
            jax.ShapeDtypeStruct((16,), jnp.int32),
            table,
            table,
        ],
        cost_estimate=BRIEF,
        compiler_params=pltpu.CompilerParams(vmem_limit_bytes=VMEM_LIMIT),
        name="cut",
    )(*operands)


def settle_kernel(*refs, layer):
    units, refs = [refs[ORDER.index(i)] for i in range(6)], refs[6:]
    q_ref, kv_ref, cos_ref, sin_ref = refs[:4]
    pool_ref, step_ref, sem = refs[-3:]
    column = lax.rem(lax.axis_index("tp"), 2)

    def copy(k, part):
        head = column if part == 0 else 1 - column
        lanes = pl.ds(pl.multiple_of(head * 2 * HD, 2 * HD), 2 * HD)
        source = units[2 * k + part].at[pl.ds(0, PROMPT), :]
        return pltpu.make_async_copy(source, pool_ref.at[k, layer, :, lanes], sem.at[2 * k + part])

    for k in range(NEAR):
        for part in range(2):
            copy(k, part).start()
    position = lax.broadcasted_iota(jnp.int32, cos_ref.shape, 0).astype(jnp.float32)
    token = lax.broadcasted_iota(jnp.int32, (GROUP, PROMPT), 1).astype(jnp.float32)
    scores, own, fresh_values = [], [], []
    for k in range(NEAR):
        held = units[max(1, 2 * k)][PROMPT : PROMPT + 1, :].astype(jnp.float32)
        held = 2.0 * held[:, :HD] + held[:, HD:]
        cosine = jnp.sum(jnp.where(position == held, cos_ref[...], 0.0), axis=0, keepdims=True)
        sine = jnp.sum(jnp.where(position == held, sin_ref[...], 0.0), axis=0, keepdims=True)
        inside = token < jnp.concatenate([held] * PAGES_P, axis=1)
        queries = q_ref[k, layer, :, :].astype(jnp.float32)
        fresh = kv_ref[k, layer, :, :].astype(jnp.float32)
        for part in range(2):
            head = column if part == 0 else 1 - column
            row = jnp.where(head == 0, queries[:1], queries[1:])
            query = jnp.concatenate([row[:, g * HD : (g + 1) * HD] for g in range(GROUP)], axis=0)
            query = rotated(query, cosine, sine).astype(jnp.bfloat16)
            mine = jnp.where(head == 0, fresh[:1], fresh[1:])
            key = jnp.broadcast_to(mine[:, :HD], (8, HD))
            key = rotated(key, cosine, sine).astype(jnp.bfloat16).astype(jnp.float32)
            cached = units[2 * k + part][:PROMPT, :HD]
            scores.append(jnp.where(inside, nt_dot(query, cached), masked_score))
            own.append(jnp.sum(query.astype(jnp.float32) * key, axis=1, keepdims=True))
            fresh_values.append(jnp.broadcast_to(mine[:, HD:], (GROUP, HD)))
    scores = jnp.concatenate(scores, axis=0)
    own = jnp.concatenate(own, axis=0)
    maximum = jnp.maximum(jnp.max(scores, axis=1, keepdims=True), own)
    exponent = jnp.exp2((scores - maximum) * EXP2_SCALE)
    own = jnp.exp2((own - maximum) * EXP2_SCALE)
    factor = 1.0 / (jnp.sum(exponent, axis=1, keepdims=True) + own)
    weights = (exponent * factor).astype(jnp.bfloat16)
    own = (own * factor).astype(jnp.bfloat16).astype(jnp.float32)
    fresh = own * jnp.concatenate(fresh_values, axis=0)
    for k in range(NEAR):
        results = []
        for part in range(2):
            rows = slice((2 * k + part) * GROUP, (2 * k + part + 1) * GROUP)
            cached = units[2 * k + part][:PROMPT, HD:]
            result = jnp.dot(weights[rows], cached, preferred_element_type=jnp.float32)
            result = result + fresh[rows]
            results.append(
                jnp.concatenate([result[g : g + 1, :] for g in range(GROUP)], axis=1)
            )
        low = jnp.where(column == 0, results[0], results[1])
        high = jnp.where(column == 0, results[1], results[0])
        both = jnp.concatenate([low, high], axis=0)
        if layer == 0:
            step_ref[k, :, :] = both
        else:
            step_ref[k, 0, :, :] = refs[4][k, :, :].astype(jnp.bfloat16)
            step_ref[k, 1, :, :] = both.astype(jnp.bfloat16)
    for k in range(NEAR):
        for part in range(2):
            copy(k, part).wait()


def settle(step_queries, step_kv, cosine, sine, units, earlier, layer):
    in_specs = [VMEM] * 10
    operands = [*(units[i] for i in ORDER), step_queries, step_kv, cosine, sine]
    aliases = {}
    step = jax.ShapeDtypeStruct((NEAR, 2, GROUP * HD), jnp.float32)
    if earlier is not None:
        pool, step_before = earlier
        in_specs += [VMEM, HBM]
        aliases = {len(operands) + 1: 0}
        operands += [step_before, pool]
        step = jax.ShapeDtypeStruct((NEAR, LAYERS, 2, GROUP * HD), jnp.bfloat16)
    return pl.pallas_call(
        functools.partial(settle_kernel, layer=layer),
        in_specs=in_specs,
        out_specs=[HBM, VMEM],
        scratch_shapes=[pltpu.SemaphoreType.DMA((2 * NEAR,))],
        out_shape=[jax.ShapeDtypeStruct((NEAR, LAYERS, PROMPT, 4 * HD), jnp.bfloat16), step],
        input_output_aliases=aliases,
        cost_estimate=BRIEF,
        compiler_params=pltpu.CompilerParams(vmem_limit_bytes=VMEM_LIMIT),
        name="settle",
    )(*operands)


def moved(value, by, flip, only=None):
    pairs = []
    for g in range(N_GRP):
        target = g ^ 1 if by is None else (g + by) % N_GRP
        for t in range(N_TP):
            pairs.append((g * N_TP + t, target * N_TP + (t ^ flip)))
    return lax.ppermute(value, ("grp", "tp"), pairs)


def on_device(
    prompt_queries, prompt_kv, page_table, prompt_lengths, targets, step_queries, step_kv
):
    tables = [jnp.asarray(table) for table in rotary_tables()]
    page_table, prompt_lengths, targets, prompt_queries, prompt_kv, *tables = (
        pltpu.with_memory_space_constraint(value, pltpu.HBM)
        for value in (
            page_table, prompt_lengths, targets.reshape(-1), prompt_queries, prompt_kv, *tables
        )
    )
    slab, plan, cosine, sine = cut(page_table, prompt_lengths, targets, prompt_kv, *tables)
    got = moved(slab, 2, 0)
    attention = functools.partial(attend, plan, prompt_queries)
    out, later_slab = attention(slab, cosine, sine, 0, 4, prompt_kv)
    later_got = moved(later_slab, 2, 0)

    local, near_first, near_other, mid_other, far_same, far_other = pack(
        plan, slab, got, cosine, sine, later_slab
    )
    far_other = moved(far_other, 1, 1)
    near_other = moved(near_other, None, 1)
    mid_other = moved(mid_other, 0, 1)
    far_same = moved(far_same, 1, 0)
    units = [None, near_other, local, mid_other, far_same, far_other]

    out, mark = attention(later_slab, cosine, sine, 4, 2, None, out, [local])
    local, near_same, near_other, mid_other, far_same, far_other, near_first = pack(
        plan, later_slab, later_got, cosine, sine, mark, [near_first]
    )
    units[0] = moved(near_first, None, 0)
    far_other = moved(far_other, 1, 1)
    near_other = moved(near_other, None, 1)
    mid_other = moved(mid_other, 0, 1)
    near_same = moved(near_same, None, 0)
    far_same = moved(far_same, 1, 0)
    later_units = [near_same, near_other, local, mid_other, far_same, far_other]
    step = functools.partial(settle, step_queries, step_kv, cosine, sine)
    earlier = step(units, None, 0)
    pool, step = step(later_units, earlier, 1)
    return out, step, pool


def solution(mesh):
    return jax.shard_map(
        on_device,
        mesh=mesh,
        in_specs=(
            P(None, "grp", "tp"),
            P(None, "grp", "tp"),
            P("grp", None),
            P("grp"),
            P("grp", None),
            P("grp", None, "tp", None),
            P("grp", None, "tp", None),
        ),
        out_specs=(P(None, "grp", "tp"), P("grp", None, "tp", None), P("grp", None, None, "tp")),
        check_vma=False,
    )
```
